256 devices in a mesh: rep: 8 (over y, x_lo), blk: 32 (over x_hi, z, core).
Axes of the slice: x: 4 (x_hi: 2, x_lo: 2; x = x_hi * 2 + x_lo), y: 4, z: 8, core: 2. Of those that a mesh axis runs over, the one named last changes fastest.
Arguments:
- features: float32 [32, 1024, 128], P('blk', 'rep'), may hold values from -6 to 6
- weight: float32 [128, 256], replicated, may hold values from -0.5 to 0.5
- cotangent: float32 [32, 1024, 256], P('blk', 'rep'), may hold values from -6 to 6
- tile_vals: float32 [32, 8, 4, 32, 128, 128], P('blk', 'rep'), may hold values from 0.002 to 0.03
- tile_rows: int32 [32, 8, 4, 32], P('blk', 'rep'), may hold values from 0 to 7, as said below
- tile_cols: int32 [32, 8, 4, 32], P('blk', 'rep'), may hold values from 0 to 7
- tile_count: int32 [32, 8, 4], P('blk', 'rep'), may hold values from 4 to 32, as said below
Outputs:
- hidden: float32 [32, 1024, 256], P('blk', 'rep')
- feature_grad: float32 [32, 1024, 128], P('blk', 'rep')
The draws below stay inside these ranges and needn't reach their ends.
Inputs may be any that keep to these rules, and one draw needn't show every extreme that they name: `tile_rows`: the 32 slots of one device and section name distinct tile positions (row, column). `tile_count`: every device has 32 live slots at some section.
All inputs are finite; a program needn't handle non-finite values.
Results may differ from the reference program's by a relative error of at most 0.0003.
Values sent between devices are 32-bit elements; how exact they have to be, the bound alone decides.
No kernel may reach another device: no remote copies, remote signals or barrier semaphores. Data moves between devices by JAX's collectives and lax.ppermute only.
A program may use at most 64 MiB of HBM per device.

```python
import math
import jax
import jax.numpy as jnp
from jax import lax

FEAT = 128
HIDDEN_SIZE = 256
BLOCK = 128
PANEL = 1024
GROUP_BLOCKS = 8
SECTIONS = 4
SLOTS = 32
N_REP = 8
N_BLK = 32


def block_positions(key):
    grid = GROUP_BLOCKS * GROUP_BLOCKS
    scores = jax.random.randint(jax.random.fold_in(key, 7), (N_BLK, N_REP, SECTIONS, grid), 0, 65536, dtype=jnp.int32)
    scores = scores * grid + jnp.arange(grid, dtype=jnp.int32)
    chosen = lax.top_k(scores, SLOTS)[1]
    return chosen.astype(jnp.int32)


def draw_tile_rows(key, part):
    return block_positions(key) // GROUP_BLOCKS


def draw_tile_cols(key, part):
    return block_positions(key) % GROUP_BLOCKS


def draw_tile_count(key, part):
    heavy = jax.random.randint(jax.random.fold_in(key, 11), (N_BLK, N_REP, 1), 1, 5, dtype=jnp.int32)
    lowest = heavy * SLOTS // 8
    highest = heavy * SLOTS // 4 + 1
    rawdraw = jax.random.randint(jax.random.fold_in(key, 12), (N_BLK, N_REP, SECTIONS), 0, 1048576, dtype=jnp.int32)
    counts = lowest + rawdraw % (highest - lowest)
    picked = jax.random.randint(jax.random.fold_in(key, 13), (N_BLK, N_REP, 1), 0, SECTIONS, dtype=jnp.int32)
    counts = jnp.where(jnp.arange(SECTIONS, dtype=jnp.int32)[None, None, :] == picked, SLOTS, counts)
    return counts.astype(jnp.int32)


def shard_levels(rng, dims, pieces, least, largest):
    def one(axis_at, blocks):
        draws = jax.random.uniform(jax.random.fold_in(jax.random.fold_in(rng, 6), axis_at), (blocks,), jnp.float32, least / len(pieces), largest / len(pieces))
        return jnp.repeat(jnp.exp(draws), dims[axis_at] // blocks).reshape((-1,) + (1,) * (len(dims) - axis_at - 1))

    level = one(*pieces[0])
    for cut in pieces[1:]:
        level = level * one(*cut)
    return level


def gaussian(rng, dims, scale, most, pieces=(), kind=jnp.bfloat16):
    loudness = shard_levels(rng, dims, pieces, -0.22, 0.18) if pieces else 1.0
    drawn = jax.random.normal(rng, dims, jnp.float32) * scale * loudness
    return jnp.minimum(jnp.maximum(drawn, -most), most).astype(kind)


def setup_inputs(seed: int = 0) -> dict:
    splits = jax.random.split(jax.random.key(seed), 8)
    return {
        "features": gaussian(splits[0], (N_BLK, PANEL, FEAT), 1.0, 6.0, ((0, 32), (1, 8)), jnp.float32),
        "weight": gaussian(splits[1], (FEAT, HIDDEN_SIZE), FEAT ** -0.5, 0.5, (), jnp.float32),
        "cotangent": gaussian(splits[2], (N_BLK, PANEL, HIDDEN_SIZE), 1.0, 6.0, ((0, 32), (1, 8)), jnp.float32),
        "tile_vals": jnp.clip(jnp.exp(math.log(0.03) - 2.70805 * jax.random.uniform(splits[3], (N_BLK, N_REP, SECTIONS, SLOTS, BLOCK, BLOCK), jnp.float32) ** shard_levels(splits[3], (N_BLK, N_REP, SECTIONS, SLOTS, BLOCK, BLOCK), ((0, 32), (1, 8)), -0.2, 0.2)), 0.002, 0.03),
        "tile_rows": draw_tile_rows(jax.random.fold_in(splits[7], 71), 0),
        "tile_cols": draw_tile_cols(jax.random.fold_in(splits[7], 71), 0),
        "tile_count": draw_tile_count(jax.random.fold_in(splits[7], 71), 0),
    }


HIGHEST = lax.Precision.HIGHEST


def forward_tiles(tile_block, row_ids, col_ids, live_count, feature_panel):
    side = tile_block.shape[-1]
    nblocks = feature_panel.shape[0] // side
    parts = feature_panel.reshape(nblocks, side, feature_panel.shape[-1])
    picked = jnp.take(parts, col_ids, axis=0)
    products = jnp.einsum("mij,mjf->mif", tile_block, picked, precision=HIGHEST)
    live_mask = (jnp.arange(tile_block.shape[0], dtype=jnp.int32) < live_count).astype(jnp.float32)
    onehot = (row_ids[None, :] == jnp.arange(nblocks, dtype=jnp.int32)[:, None]).astype(jnp.float32) * live_mask[None, :]
    return jnp.einsum("gm,mif->gif", onehot, products, precision=HIGHEST).reshape(feature_panel.shape)


def backward_tiles(tile_block, row_ids, col_ids, live_count, grad_panel):
    side = tile_block.shape[-1]
    nblocks = grad_panel.shape[0] // side
    parts = grad_panel.reshape(nblocks, side, grad_panel.shape[-1])
    picked = jnp.take(parts, row_ids, axis=0)
    products = jnp.einsum("mji,mjf->mif", tile_block, picked, precision=HIGHEST)
    live_mask = (jnp.arange(tile_block.shape[0], dtype=jnp.int32) < live_count).astype(jnp.float32)
    onehot = (col_ids[None, :] == jnp.arange(nblocks, dtype=jnp.int32)[:, None]).astype(jnp.float32) * live_mask[None, :]
    return jnp.einsum("gm,mif->gif", onehot, products, precision=HIGHEST).reshape(grad_panel.shape)


def reference(features, weight, cotangent, tile_vals, tile_rows, tile_cols, tile_count):
    groups = features.shape[0]
    steps_all = N_REP * SECTIONS

    def group_forward(group):
        def add_section(index, partial_value):
            replica = index // SECTIONS
            step = index % SECTIONS
            source = (group + index) % groups
            term = forward_tiles(tile_vals[group, replica, step], tile_rows[group, replica, step],
                                 tile_cols[group, replica, step], tile_count[group, replica, step], features[source])
            return partial_value + term
        return lax.fori_loop(0, steps_all, add_section, jnp.zeros(features.shape[1:], features.dtype))

    propagated = lax.map(group_forward, jnp.arange(groups, dtype=jnp.int32))
    preact = jnp.einsum("bnf,fh->bnh", propagated, weight, precision=HIGHEST)
    sigmoid_pre = jax.nn.sigmoid(preact)
    hidden = preact * sigmoid_pre
    grad_pre = cotangent * sigmoid_pre * (1.0 + preact * (1.0 - sigmoid_pre))
    grad_prop = jnp.einsum("bnh,fh->bnf", grad_pre, weight, precision=HIGHEST)

    def group_backward(group, totals):
        def add_section(index, inner_totals):
            replica = index // SECTIONS
            step = index % SECTIONS
            target = (group + index) % groups
            term = backward_tiles(tile_vals[group, replica, step], tile_rows[group, replica, step],
                                  tile_cols[group, replica, step], tile_count[group, replica, step], grad_prop[group])
            return inner_totals.at[target].add(term)
        return lax.fori_loop(0, steps_all, add_section, totals)

    feature_grad = lax.fori_loop(0, groups, group_backward, jnp.zeros(features.shape, features.dtype))
    return hidden, feature_grad
```

```python
import functools

import jax
import jax.numpy as jnp
from jax import lax
from jax.experimental import pallas as pl
from jax.experimental.pallas import tpu as pltpu
from jax.sharding import PartitionSpec as P

F32 = jnp.float32
BF16 = jnp.bfloat16
HIGHEST = lax.Precision.HIGHEST
SIDE = 128
CHUNK = 8


def halves(value):
    high = value.astype(BF16)
    return high, (value - high.astype(F32)).astype(BF16)


def store_split(split, block, value):
    high, low = halves(value)
    split[block, :SIDE, :SIDE] = high
    split[block, SIDE:, :SIDE] = high
    split[block, :SIDE, SIDE:] = low
    split[block, SIDE:, SIDE:] = low


def clear(total):
    total[...] = jnp.zeros_like(total)


def forward_body(n_in, nblocks, has_start, choose, place, rows, cols, count, *refs):
    panels = refs[:n_in]
    tiles = refs[n_in]
    start = refs[n_in + 1] if has_start else None
    out, split, total = refs[-3:]
    part, chunk = pl.program_id(0), pl.program_id(1)
    section = place[part]

    @pl.when((part == 0) & (chunk == 0))
    def _():
        clear(total)

    for index in range(n_in - int(choose)):
        @pl.when((part == index) & (chunk == 0))
        def _(index=index):
            for block in range(nblocks):
                at = pl.ds(block * SIDE, SIDE)
                value = panels[index][at, :]
                if choose and index == n_in - 2:
                    value = jnp.where(place[3] == 0, value, panels[index + 1][at, :])
                store_split(split, block, value)

    for slot in range(CHUNK):
        number = chunk * CHUNK + slot
        row = jnp.where(number < count[section], rows[section, number], nblocks)
        col = cols[section, number] ^ place[2]
        left = jnp.concatenate(halves(tiles[0, slot]), axis=1)
        product = jnp.dot(left, split[col], preferred_element_type=F32)
        at = pl.ds(pl.multiple_of(row * SIDE, SIDE), SIDE)
        total[at, :] += product

    @pl.when((part == pl.num_programs(0) - 1) & (chunk == pl.num_programs(1) - 1))
    def _():
        live = pl.ds(0, nblocks * SIDE)
        value = total[live, :SIDE] + total[live, SIDE:]
        out[...] = value + start[...] if has_start else value


def forward_tiles(place, rows, cols, count, panels, tiles, start, choose):
    slots, nodes, features = tiles.shape[1], panels[0].shape[0], panels[0].shape[1]
    nblocks = nodes // SIDE
    parts = len(panels) - int(choose)
    whole = pl.BlockSpec((nodes, features), lambda i, j, *_: (0, 0))
    extra = [] if start is None else [start]
    return pl.pallas_call(
        functools.partial(forward_body, len(panels), nblocks, start is not None, choose),
        grid_spec=pltpu.PrefetchScalarGridSpec(
            num_scalar_prefetch=4,
            grid=(parts, slots // CHUNK),
            in_specs=[whole] * len(panels)
            + [pl.BlockSpec((1, CHUNK, SIDE, SIDE), lambda i, j, place, *_: (place[i], j, 0, 0))]
            + [whole] * len(extra),
            out_specs=whole,
            scratch_shapes=[
                pltpu.VMEM((nblocks, 2 * SIDE, 2 * SIDE), BF16),
                pltpu.VMEM((nodes + SIDE, 2 * features), F32),
            ],
        ),
        out_shape=jax.ShapeDtypeStruct((nodes, features), F32),
        compiler_params=pltpu.CompilerParams(vmem_limit_bytes=24 << 20),
        cost_estimate=pl.CostEstimate(
            flops=12 * parts * slots * SIDE * SIDE * features,
            bytes_accessed=4 * parts * slots * SIDE * SIDE,
            transcendentals=0,
        ),
    )(place, rows, cols, count, *panels, tiles, *extra)


def backward_body(parts, nblocks, place, rows, cols, count, panel, tiles, *refs):
    outs = refs[:parts]
    split, total = refs[parts:]
    part, chunk = pl.program_id(0), pl.program_id(1)
    section = place[part]

    @pl.when((part == 0) & (chunk == 0))
    def _():
        for block in range(nblocks):
            store_split(split, block, panel[pl.ds(block * SIDE, SIDE), :])

    @pl.when(chunk == 0)
    def _():
        clear(total)

    for slot in range(CHUNK):
        number = chunk * CHUNK + slot
        row = rows[section, number]
        col = jnp.where(number < count[section], cols[section, number] ^ place[2], nblocks)
        left = jnp.concatenate(halves(tiles[0, slot].T), axis=1)
        product = jnp.dot(left, split[row], preferred_element_type=F32)
        at = pl.ds(pl.multiple_of(col * SIDE, SIDE), SIDE)
        total[at, :] += product

    for index in range(parts):
        @pl.when((part == index) & (chunk == pl.num_programs(1) - 1))
        def _(index=index):
            live = pl.ds(0, nblocks * SIDE)
            outs[index][...] = total[live, :SIDE] + total[live, SIDE:]


def backward_tiles(place, rows, cols, count, panel, tiles, parts):
    slots, nodes, features = tiles.shape[1], panel.shape[0], panel.shape[1]
    nblocks = nodes // SIDE
    whole = pl.BlockSpec((nodes, features), lambda i, j, *_: (0, 0))
    return pl.pallas_call(
        functools.partial(backward_body, parts, nblocks),
        grid_spec=pltpu.PrefetchScalarGridSpec(
            num_scalar_prefetch=4,
            grid=(parts, slots // CHUNK),
            in_specs=[
                whole,
                pl.BlockSpec((1, CHUNK, SIDE, SIDE), lambda i, j, place, *_: (place[i], j, 0, 0)),
            ],
            out_specs=[whole] * parts,
            scratch_shapes=[
                pltpu.VMEM((nblocks, 2 * SIDE, 2 * SIDE), BF16),
                pltpu.VMEM((nodes + SIDE, 2 * features), F32),
            ],
        ),
        out_shape=[jax.ShapeDtypeStruct((nodes, features), F32)] * parts,
        compiler_params=pltpu.CompilerParams(vmem_limit_bytes=24 << 20),
        cost_estimate=pl.CostEstimate(
            flops=12 * parts * slots * SIDE * SIDE * features,
            bytes_accessed=4 * parts * slots * SIDE * SIDE,
            transcendentals=0,
        ),
    )(place, rows, cols, count, panel, tiles)


def dense_body(partials, weight, cotangent, hidden, spread):
    propagated = partials[0]
    for index in range(1, partials.shape[0]):
        propagated = propagated + partials[index]
    preact = jnp.dot(propagated, weight[...], precision=HIGHEST, preferred_element_type=F32)
    gate = 1.0 / (1.0 + jnp.exp(-preact))
    hidden[...] = preact * gate
    grad_pre = cotangent[...] * gate * (1.0 + preact * (1.0 - gate))
    grad = lax.dot_general(
        grad_pre, weight[...], (((1,), (1,)), ((), ())),
        precision=HIGHEST, preferred_element_type=F32,
    )
    for index in range(spread.shape[0]):
        spread[index] = grad


def dense(partials, weight, cotangent):
    return pl.pallas_call(
        dense_body,
        out_shape=[
            jax.ShapeDtypeStruct(cotangent.shape, F32),
            jax.ShapeDtypeStruct(partials.shape, F32),
        ],
    )(partials, weight, cotangent)


def shards(features, weight, cotangent, tile_vals, tile_rows, tile_cols, tile_count):
    replicas, groups = lax.axis_size("rep"), lax.axis_size("blk")
    sections = groups // replicas
    rep = lax.axis_index("rep")
    core = lax.axis_index("blk") % 2
    tiles, rows, cols, count = tile_vals[0, 0], tile_rows[0, 0], tile_cols[0, 0], tile_count[0, 0]
    near = jnp.stack([jnp.int32(2), 3 - 2 * core, rep, core]).astype(jnp.int32)
    far = jnp.stack([jnp.int32(0), 1 + 2 * core, rep, core]).astype(jnp.int32)
    fars = jnp.stack([1 + 2 * core, jnp.int32(0), rep, core]).astype(jnp.int32)

    def device(group, replica):
        return replica * groups + group % groups

    def joint(block, source):
        return lax.ppermute(
            block, ("rep", "blk"),
            [(device(*source(g, r)), device(g, r)) for r in range(replicas) for g in range(groups)],
        )

    def back(block, target):
        return lax.ppermute(
            block, ("rep", "blk"),
            [(device(g, r), device(*target(g, r))) for r in range(replicas) for g in range(groups)],
        )

    def along(block, distance, ids):
        return lax.ppermute(block, "blk", [(g, (g + distance) % groups) for g in ids])

    everyone, evens, odds = range(groups), range(0, groups, 2), range(1, groups, 2)
    twin = [(r ^ 1, r) for r in range(replicas)]
    swap = [(g ^ 1, g) for g in range(groups)]

    own = features[0]
    pair = jnp.concatenate([own, lax.ppermute(own, "rep", twin)])
    base = jnp.concatenate(
        [
            joint(pair, lambda g, r, k=k: (g + sections * r + 2, r ^ (2 * k)))
            for k in range(replicas // 2)
        ]
    )
    lower = along(base, 2, everyone)
    upper = along(base, -1, evens)
    beside = lax.ppermute(base, "blk", swap)
    partial_sum = forward_tiles(near, rows, cols, count, [base, beside], tiles, None, False)
    lower_beside = along(lower, -1, odds)
    partial_sum = forward_tiles(
        far, rows, cols, count, [lower, lower_beside, upper], tiles, partial_sum, True
    )
    partials = lax.all_to_all(
        partial_sum.reshape(replicas, -1, own.shape[-1]), "rep", 0, 0, tiled=True
    )
    hidden, spread = dense(partials, weight, cotangent[0])
    grad_panel = lax.all_to_all(spread, "rep", 0, 0, tiled=True).reshape(base.shape)
    (outer,) = backward_tiles(fars, rows, cols, count, grad_panel, tiles, 1)
    outer_in = along(outer, 1, evens)
    to_lower = along(outer, 1, odds)
    (lowest,) = backward_tiles(far, rows, cols, count, grad_panel, tiles, 1)
    from_upper = along(lowest + outer_in, -2, everyone)
    mine, other = backward_tiles(near, rows, cols, count, grad_panel, tiles, 2)
    total = mine + lax.ppermute(other, "blk", swap) + from_upper + to_lower
    parts = total.reshape(replicas // 2, -1, own.shape[-1])
    pair_sum = sum(
        back(parts[k], lambda g, r, k=k: (g + sections * r + 2, r ^ (2 * k)))
        for k in range(replicas // 2)
    )
    kept, sent = jnp.split(pair_sum, 2)
    feature_grad = kept + lax.ppermute(sent, "rep", twin)
    return hidden[None], feature_grad[None]


def solution(mesh):
    placed = (
        P("blk", "rep", None),
        P(),
        P("blk", "rep", None),
        P("blk", "rep", None, None, None, None),
        P("blk", "rep", None, None),
        P("blk", "rep", None, None),
        P("blk", "rep", None),
    )
    return jax.shard_map(
        shards,
        mesh=mesh,
        in_specs=placed,
        out_specs=(P("blk", "rep", None), P("blk", "rep", None)),
        check_vma=False,
    )
```

```python
import functools

import jax
import jax.numpy as jnp
from jax import lax
from jax.experimental import pallas as pl
from jax.experimental.pallas import tpu as pltpu
from jax.sharding import PartitionSpec as P

F32 = jnp.float32
BF16 = jnp.bfloat16
HIGHEST = lax.Precision.HIGHEST
SIDE = 128
CHUNK = 8
NEAR, FAR, OUTER, LOWEST, CORE = 0, 2, 3, 2, 4


def halves(value):
    high = value.astype(BF16)
    return high, (value - high.astype(F32)).astype(BF16)


def store_split(split, block, value):
    high, low = halves(value)
    split[block, :SIDE, :SIDE] = high
    split[block, SIDE:, :SIDE] = high
    split[block, :SIDE, SIDE:] = low
    split[block, SIDE:, SIDE:] = low


def tile_copies(parts, first, info, tiles, held, sems):
    chunks = held.shape[1] // CHUNK

    def copy(part, chunk):
        at = pl.ds(pl.multiple_of(chunk * CHUNK, CHUNK), CHUNK)
        return pltpu.make_async_copy(
            tiles.at[info[0, first + part], at], held.at[part, at], sems.at[part, chunk]
        )

    for part in range(parts):
        for chunk in range(chunks):
            copy(part, chunk).start()
    return copy, chunks


def multiply(part, section, copy, chunks, info, source, target, transposed, held, split, total):
    @pl.loop(0, chunks)
    def _(chunk):
        copy(part, chunk).wait()
        for slot in range(CHUNK):
            number = chunk * CHUNK + slot
            tile = held[part, number]
            left = jnp.concatenate(halves(tile.T if transposed else tile), axis=1)
            right = split[info[source + section, number]]
            product = jnp.dot(left, right, preferred_element_type=F32)
            row = info[target + section, number] * SIDE
            total[pl.ds(pl.multiple_of(row, SIDE), SIDE), :] += product


def folded(total, nodes):
    live = pl.ds(0, nodes)
    return total[live, :SIDE] + total[live, SIDE:]


def forward_body(n_in, has_start, choose, first, info, *refs):
    panels, tiles = refs[:n_in], refs[n_in]
    out, split, total, held, sems = refs[-5:]
    nodes, parts = out.shape[0], n_in - int(choose)
    sections = info.shape[0] // 4
    copy, chunks = tile_copies(parts, first, info, tiles, held, sems)
    total[...] = jnp.zeros_like(total)
    for part in range(parts):
        for block in range(nodes // SIDE):
            at = pl.ds(block * SIDE, SIDE)
            value = panels[part][at, :]
            if choose and part == parts - 1:
                value = jnp.where(info[0, CORE] == 0, value, panels[parts][at, :])
            store_split(split, block, value)
        multiply(
            part, info[0, first + part], copy, chunks, info, 1 + sections, 1, False,
            held, split, total,
        )
    value = folded(total, nodes)
    out[...] = value + refs[n_in + 1][...] if has_start else value


def backward_body(parts, first, info, panel, tiles, *refs):
    outs = refs[:parts]
    split, total, held, sems = refs[parts:]
    nodes = panel.shape[0]
    sections = info.shape[0] // 4
    copy, chunks = tile_copies(parts, first, info, tiles, held, sems)
    for block in range(nodes // SIDE):
        store_split(split, block, panel[pl.ds(block * SIDE, SIDE), :])
    for part in range(parts):
        total[...] = jnp.zeros_like(total)
        multiply(
            part, info[0, first + part], copy, chunks, info, 1 + 2 * sections, 1 + 3 * sections,
            True, held, split, total,
        )
        outs[part][...] = folded(total, nodes)


def tile_call(body, parts, info, panels, tiles, extra, n_out, cost):
    slots, (nodes, features) = tiles.shape[1], panels[0].shape
    whole = pl.BlockSpec(memory_space=pltpu.VMEM)
    return pl.pallas_call(
        body,
        in_specs=[pl.BlockSpec(memory_space=pltpu.SMEM)]
        + [whole] * len(panels)
        + [pl.BlockSpec(memory_space=pltpu.HBM)]
        + [whole] * len(extra),
        out_specs=[whole] * n_out,
        scratch_shapes=[
            pltpu.VMEM((nodes // SIDE, 2 * SIDE, 2 * SIDE), BF16),
            pltpu.VMEM((nodes + SIDE, 2 * features), F32),
            pltpu.VMEM((parts, slots, SIDE, SIDE), F32),
            pltpu.SemaphoreType.DMA((parts, slots // CHUNK)),
        ],
        out_shape=[jax.ShapeDtypeStruct((nodes, features), F32)] * n_out,
        compiler_params=pltpu.CompilerParams(vmem_limit_bytes=50 << 20),
        cost_estimate=pl.CostEstimate(
            flops=cost * parts * slots * SIDE * SIDE * features,
            bytes_accessed=4 * parts * slots * SIDE * SIDE,
            transcendentals=0,
        ),
    )(info, *panels, tiles, *extra)


def forward_tiles(first, info, panels, tiles, start, choose):
    extra = [] if start is None else [start]
    body = functools.partial(forward_body, len(panels), start is not None, choose, first)
    return tile_call(body, len(panels) - int(choose), info, panels, tiles, extra, 1, 32)[0]


def backward_tiles(first, info, panel, tiles, parts, cost=32):
    body = functools.partial(backward_body, parts, first)
    return tile_call(body, parts, info, [panel], tiles, [], parts, cost)


def dense_body(partials, weight, cotangent, hidden, spread):
    propagated = partials[0]
    for index in range(1, partials.shape[0]):
        propagated = propagated + partials[index]
    preact = jnp.dot(propagated, weight[...], precision=HIGHEST, preferred_element_type=F32)
    gate = 1.0 / (1.0 + jnp.exp(-preact))
    hidden[...] = preact * gate
    grad_pre = cotangent[...] * gate * (1.0 + preact * (1.0 - gate))
    grad = lax.dot_general(
        grad_pre, weight[...], (((1,), (1,)), ((), ())),
        precision=HIGHEST, preferred_element_type=F32,
    )
    for index in range(spread.shape[0]):
        spread[index] = grad


def dense(partials, weight, cotangent):
    return pl.pallas_call(
        dense_body,
        out_shape=[
            jax.ShapeDtypeStruct(cotangent.shape, F32),
            jax.ShapeDtypeStruct(partials.shape, F32),
        ],
    )(partials, weight, cotangent)


def shards(features, weight, cotangent, tile_vals, tile_rows, tile_cols, tile_count):
    replicas, groups = lax.axis_size("rep"), lax.axis_size("blk")
    sections = groups // replicas
    rep = lax.axis_index("rep")
    core = lax.axis_index("blk") % 2
    tiles, rows, cols, count = tile_vals[0, 0], tile_rows[0, 0], tile_cols[0, 0], tile_count[0, 0]
    slots = rows.shape[-1]
    live = lax.broadcasted_iota(jnp.int32, rows.shape, 1) < count[:, None]
    lane = lax.broadcasted_iota(jnp.int32, (1, slots), 1)
    plan = jnp.where(lane == 0, 2, 0)
    plan = jnp.where(lane == 1, 3 - 2 * core, plan)
    plan = jnp.where(lane == 3, 1 + 2 * core, plan)
    plan = jnp.where(lane == CORE, core, plan)
    spare = replicas
    info = jnp.concatenate(
        [plan, jnp.where(live, rows, spare), cols ^ rep, rows, jnp.where(live, cols ^ rep, spare)]
    )

    def device(group, replica):
        return replica * groups + group % groups

    def joint(block, source):
        return lax.ppermute(
            block, ("rep", "blk"),
            [(device(*source(g, r)), device(g, r)) for r in range(replicas) for g in range(groups)],
        )

    def back(block, target):
        return lax.ppermute(
            block, ("rep", "blk"),
            [(device(g, r), device(*target(g, r))) for r in range(replicas) for g in range(groups)],
        )

    def along(block, distance, ids):
        return lax.ppermute(block, "blk", [(g, (g + distance) % groups) for g in ids])

    everyone, evens, odds = range(groups), range(0, groups, 2), range(1, groups, 2)
    twin = [(r ^ 1, r) for r in range(replicas)]
    swap = [(g ^ 1, g) for g in range(groups)]

    own = features[0]
    nodes = own.shape[0]
    pair = lax.dynamic_update_slice(
        jnp.concatenate([own, own]), lax.ppermute(own, "rep", twin), (nodes, 0)
    )
    base = jnp.concatenate(
        [
            joint(pair, lambda g, r, k=k: (g + sections * r + 2, r ^ (2 * k)))
            for k in range(replicas // 2)
        ]
    )
    lower = along(base, 2, everyone)
    upper = along(base, -1, evens)
    beside = lax.ppermute(base, "blk", swap)
    partial_sum = forward_tiles(NEAR, info, [base, beside], tiles, None, False)
    lower, partial_sum = lax.optimization_barrier((lower, partial_sum))
    lower_beside = along(lower, -1, odds)
    partial_sum = forward_tiles(
        FAR, info, [lower, lower_beside, upper], tiles, partial_sum, True
    )
    partials = lax.all_to_all(
        partial_sum.reshape(replicas, -1, own.shape[-1]), "rep", 0, 0, tiled=True
    )
    hidden, spread = dense(partials, weight, cotangent[0])
    grad_panel = lax.all_to_all(spread, "rep", 0, 0, tiled=True).reshape(base.shape)
    (outer,) = backward_tiles(OUTER, info, grad_panel, tiles, 1)
    outer_in = along(outer, 1, evens)
    to_lower = along(outer, 1, odds)
    (lowest,) = backward_tiles(LOWEST, info, grad_panel, tiles, 1)
    combined = lowest + outer_in
    from_upper = along(combined, -2, everyone)
    late_panel, _ = lax.optimization_barrier((grad_panel, combined))
    mine, other = backward_tiles(NEAR, info, late_panel, tiles, 2)
    other, from_upper = lax.optimization_barrier((other, from_upper))
    total = mine + lax.ppermute(other, "blk", swap) + from_upper + to_lower
    parts = total.reshape(replicas // 2, -1, own.shape[-1])
    pair_sum = 0.0
    for k in range(replicas // 2):
        part = parts[k]
        if k:
            part = lax.ppermute(part, "rep", [(r, r ^ (2 * k)) for r in range(replicas)])
        pair_sum = pair_sum + back(
            part, lambda g, r, k=k: (g + sections * (r ^ (2 * k)) + 2, r)
        )
    kept, sent = jnp.split(pair_sum, 2)
    feature_grad = kept + lax.ppermute(sent, "rep", twin)
    return hidden[None], feature_grad[None]


def solution(mesh):
    placed = (
        P("blk", "rep", None),
        P(),
        P("blk", "rep", None),
        P("blk", "rep", None, None, None, None),
        P("blk", "rep", None, None),
        P("blk", "rep", None, None),
        P("blk", "rep", None),
    )
    return jax.shard_map(
        shards,
        mesh=mesh,
        in_specs=placed,
        out_specs=(P("blk", "rep", None), P("blk", "rep", None)),
        check_vma=False,
    )
```

```python
import functools

import jax
import jax.numpy as jnp
from jax import lax
from jax.experimental import pallas as pl
from jax.experimental.pallas import tpu as pltpu
from jax.sharding import PartitionSpec as P

F32 = jnp.float32
BF16 = jnp.bfloat16
HIGHEST = lax.Precision.HIGHEST
SIDE = 128
CHUNK = 16
NEAR, FAR, OUTER, LOWEST, CORE = 0, 2, 3, 2, 4


def halves(value):
    high = value.astype(BF16)
    return high, (value - high.astype(F32)).astype(BF16)


def store_split(split, block, value):
    high, low = halves(value)
    split[block, :SIDE, :SIDE] = high
    split[block, SIDE:, :SIDE] = high
    split[block, :SIDE, SIDE:] = low
    split[block, SIDE:, SIDE:] = low


def tile_copies(parts, first, info, tiles, held, sems):
    chunks = held.shape[1] // CHUNK

    def copy(part, chunk):
        at = pl.ds(pl.multiple_of(chunk * CHUNK, CHUNK), CHUNK)
        return pltpu.make_async_copy(
            tiles.at[info[0, first + part], at], held.at[part, at], sems.at[part, chunk]
        )

    for part in range(parts):
        for chunk in range(chunks):
            copy(part, chunk).start()
    return copy, chunks


def multiply(part, section, copy, chunks, info, source, target, transposed, held, split, total):
    @pl.loop(0, chunks)
    def _(chunk):
        copy(part, chunk).wait()
        for slot in range(CHUNK):
            number = chunk * CHUNK + slot
            tile = held[part, number]
            left = jnp.concatenate(halves(tile.T if transposed else tile), axis=1)
            right = split[info[source + section, number]]
            product = jnp.dot(left, right, preferred_element_type=F32)
            row = info[target + section, number] * SIDE
            total[pl.ds(pl.multiple_of(row, SIDE), SIDE), :] += product


def folded(total, nodes):
    live = pl.ds(0, nodes)
    return total[live, :SIDE] + total[live, SIDE:]


def forward_body(n_in, has_start, choose, first, info, *refs):
    panels, tiles = refs[:n_in], refs[n_in]
    out, split, total, held, sems = refs[-5:]
    nodes, parts = out.shape[0], n_in - int(choose)
    sections = info.shape[0] // 4
    copy, chunks = tile_copies(parts, first, info, tiles, held, sems)
    total[...] = jnp.zeros_like(total)
    for part in range(parts):
        for block in range(nodes // SIDE):
            at = pl.ds(block * SIDE, SIDE)
            value = panels[part][at, :]
            if choose and part == parts - 1:
                value = jnp.where(info[0, CORE] == 0, value, panels[parts][at, :])
            store_split(split, block, value)
        multiply(
            part, info[0, first + part], copy, chunks, info, 1 + sections, 1, False,
            held, split, total,
        )
    value = folded(total, nodes)
    out[...] = value + refs[n_in + 1][...] if has_start else value


def backward_body(parts, first, info, panel, tiles, *refs):
    outs = refs[:parts]
    split, total, held, sems = refs[parts:]
    nodes = panel.shape[0]
    sections = info.shape[0] // 4
    copy, chunks = tile_copies(parts, first, info, tiles, held, sems)
    for block in range(nodes // SIDE):
        store_split(split, block, panel[pl.ds(block * SIDE, SIDE), :])
    for part in range(parts):
        total[...] = jnp.zeros_like(total)
        multiply(
            part, info[0, first + part], copy, chunks, info, 1 + 2 * sections, 1 + 3 * sections,
            True, held, split, total,
        )
        outs[part][...] = folded(total, nodes)


def tile_call(body, parts, info, panels, tiles, extra, n_out, cost):
    slots, (nodes, features) = tiles.shape[1], panels[0].shape
    whole = pl.BlockSpec(memory_space=pltpu.VMEM)
    return pl.pallas_call(
        body,
        in_specs=[pl.BlockSpec(memory_space=pltpu.SMEM)]
        + [whole] * len(panels)
        + [pl.BlockSpec(memory_space=pltpu.HBM)]
        + [whole] * len(extra),
        out_specs=[whole] * n_out,
        scratch_shapes=[
            pltpu.VMEM((nodes // SIDE, 2 * SIDE, 2 * SIDE), BF16),
            pltpu.VMEM((nodes + SIDE, 2 * features), F32),
            pltpu.VMEM((parts, slots, SIDE, SIDE), F32),
            pltpu.SemaphoreType.DMA((parts, slots // CHUNK)),
        ],
        out_shape=[jax.ShapeDtypeStruct((nodes, features), F32)] * n_out,
        compiler_params=pltpu.CompilerParams(vmem_limit_bytes=50 << 20),
        cost_estimate=pl.CostEstimate(
            flops=cost * parts * slots * SIDE * SIDE * features,
            bytes_accessed=4 * parts * slots * SIDE * SIDE,
            transcendentals=0,
        ),
    )(info, *panels, tiles, *extra)


def forward_tiles(first, info, panels, tiles, start, choose):
    extra = [] if start is None else [start]
    body = functools.partial(forward_body, len(panels), start is not None, choose, first)
    return tile_call(body, len(panels) - int(choose), info, panels, tiles, extra, 1, 32)[0]


def backward_tiles(first, info, panel, tiles, parts, cost=32):
    body = functools.partial(backward_body, parts, first)
    return tile_call(body, parts, info, [panel], tiles, [], parts, cost)


def dense_body(partials, weight, cotangent, hidden, spread):
    propagated = partials[0]
    for index in range(1, partials.shape[0]):
        propagated = propagated + partials[index]
    preact = jnp.dot(propagated, weight[...], precision=HIGHEST, preferred_element_type=F32)
    gate = 1.0 / (1.0 + jnp.exp(-preact))
    hidden[...] = preact * gate
    grad_pre = cotangent[...] * gate * (1.0 + preact * (1.0 - gate))
    grad = lax.dot_general(
        grad_pre, weight[...], (((1,), (1,)), ((), ())),
        precision=HIGHEST, preferred_element_type=F32,
    )
    for index in range(spread.shape[0]):
        spread[index] = grad


def dense(partials, weight, cotangent):
    return pl.pallas_call(
        dense_body,
        out_shape=[
            jax.ShapeDtypeStruct(cotangent.shape, F32),
            jax.ShapeDtypeStruct(partials.shape, F32),
        ],
    )(partials, weight, cotangent)


def shards(features, weight, cotangent, tile_vals, tile_rows, tile_cols, tile_count):
    replicas, groups = lax.axis_size("rep"), lax.axis_size("blk")
    sections = groups // replicas
    rep = lax.axis_index("rep")
    core = lax.axis_index("blk") % 2
    tiles, rows, cols, count = tile_vals[0, 0], tile_rows[0, 0], tile_cols[0, 0], tile_count[0, 0]
    slots = rows.shape[-1]
    live = lax.broadcasted_iota(jnp.int32, rows.shape, 1) < count[:, None]
    lane = lax.broadcasted_iota(jnp.int32, (1, slots), 1)
    plan = jnp.where(lane == 0, 2, 0)
    plan = jnp.where(lane == 1, 3 - 2 * core, plan)
    plan = jnp.where(lane == 3, 1 + 2 * core, plan)
    plan = jnp.where(lane == CORE, core, plan)
    spare = replicas
    info = jnp.concatenate(
        [plan, jnp.where(live, rows, spare), cols ^ rep, rows, jnp.where(live, cols ^ rep, spare)]
    )

    def device(group, replica):
        return replica * groups + group % groups

    def joint(block, source):
        return lax.ppermute(
            block, ("rep", "blk"),
            [(device(*source(g, r)), device(g, r)) for r in range(replicas) for g in range(groups)],
        )

    def back(block, target):
        return lax.ppermute(
            block, ("rep", "blk"),
            [(device(g, r), device(*target(g, r))) for r in range(replicas) for g in range(groups)],
        )

    def along(block, distance, ids):
        return lax.ppermute(block, "blk", [(g, (g + distance) % groups) for g in ids])

    everyone, evens, odds = range(groups), range(0, groups, 2), range(1, groups, 2)
    twin = [(r ^ 1, r) for r in range(replicas)]
    swap = [(g ^ 1, g) for g in range(groups)]

    own = features[0]
    nodes = own.shape[0]
    pair = lax.dynamic_update_slice(
        jnp.concatenate([own, own]), lax.ppermute(own, "rep", twin), (nodes, 0)
    )
    pair, info = lax.optimization_barrier((pair, info))
    base = jnp.concatenate(
        [
            joint(pair, lambda g, r, k=k: (g + sections * r + 2, r ^ (2 * k)))
            for k in range(replicas // 2)
        ]
    )
    lower = along(base, 2, everyone)
    upper = along(base, -1, evens)
    beside = lax.ppermute(base, "blk", swap)
    partial_sum = forward_tiles(NEAR, info, [base, beside], tiles, None, False)
    lower, partial_sum = lax.optimization_barrier((lower, partial_sum))
    lower_beside = along(lower, -1, odds)
    partial_sum = forward_tiles(FAR, info, [lower], tiles, partial_sum, False)
    partial_sum = forward_tiles(
        OUTER, info, [lower_beside, upper], tiles, partial_sum, True
    )
    partials = lax.all_to_all(
        partial_sum.reshape(replicas, -1, own.shape[-1]), "rep", 0, 0, tiled=True
    )
    hidden, spread = dense(partials, weight, cotangent[0])
    grad_panel = lax.all_to_all(spread, "rep", 0, 0, tiled=True).reshape(base.shape)
    (outer,) = backward_tiles(OUTER, info, grad_panel, tiles, 1)
    outer_in = along(outer, 1, evens)
    to_lower = along(outer, 1, odds)
    (lowest,) = backward_tiles(LOWEST, info, grad_panel, tiles, 1)
    combined = lowest + outer_in
    from_upper = along(combined, -2, everyone)
    late_panel, _ = lax.optimization_barrier((grad_panel, combined))
    (other,) = backward_tiles(NEAR + 1, info, late_panel, tiles, 1)
    late_panel, other = lax.optimization_barrier((late_panel, other))
    (mine,) = backward_tiles(NEAR, info, late_panel, tiles, 1)
    received = lax.optimization_barrier(mine + from_upper + to_lower)
    total = received + lax.ppermute(other, "blk", swap)
    parts = total.reshape(replicas // 2, -1, own.shape[-1])
    pair_sum = 0.0
    for k in range(replicas // 2):
        part = parts[k]
        if k:
            part = lax.ppermute(part, "rep", [(r, r ^ (2 * k)) for r in range(replicas)])
        pair_sum = pair_sum + back(
            part, lambda g, r, k=k: (g + sections * (r ^ (2 * k)) + 2, r)
        )
    kept, sent = jnp.split(pair_sum, 2)
    feature_grad = kept + lax.ppermute(sent, "rep", twin)
    return hidden[None], feature_grad[None]


def solution(mesh):
    placed = (
        P("blk", "rep", None),
        P(),
        P("blk", "rep", None),
        P("blk", "rep", None, None, None, None),
        P("blk", "rep", None, None),
        P("blk", "rep", None, None),
        P("blk", "rep", None),
    )
    return jax.shard_map(
        shards,
        mesh=mesh,
        in_specs=placed,
        out_specs=(P("blk", "rep", None), P("blk", "rep", None)),
        check_vma=False,
    )
```

```python
import functools

import jax
import jax.numpy as jnp
from jax import lax
from jax.experimental import pallas as pl
from jax.experimental.pallas import tpu as pltpu
from jax.sharding import PartitionSpec as P

F32 = jnp.float32
BF16 = jnp.bfloat16
HIGHEST = lax.Precision.HIGHEST
SIDE = 128
CHUNK = 16
NEAR, FAR, OUTER, LOWEST, CORE = 0, 2, 3, 2, 4


def halves(value):
    high = value.astype(BF16)
    return high, (value - high.astype(F32)).astype(BF16)


def store_split(split, block, value):
    high, low = halves(value)
    split[block, :SIDE, :SIDE] = high
    split[block, SIDE:, :SIDE] = high
    split[block, :SIDE, SIDE:] = low
    split[block, SIDE:, SIDE:] = low


def tile_copies(parts, first, info, tiles, held, sems):
    chunks = held.shape[1] // CHUNK

    def copy(part, chunk):
        at = pl.ds(pl.multiple_of(chunk * CHUNK, CHUNK), CHUNK)
        return pltpu.make_async_copy(
            tiles.at[info[0, first + part], at], held.at[part, at], sems.at[part, chunk]
        )

    for part in range(parts):
        for chunk in range(chunks):
            copy(part, chunk).start()
    return copy, chunks


def multiply(part, section, copy, chunks, info, source, target, transposed, held, split, total):
    @pl.loop(0, chunks)
    def _(chunk):
        copy(part, chunk).wait()
        for slot in range(CHUNK):
            number = chunk * CHUNK + slot
            tile = held[part, number]
            left = jnp.concatenate(halves(tile.T if transposed else tile), axis=1)
            right = split[info[source + section, number]]
            product = jnp.dot(left, right, preferred_element_type=F32)
            row = info[target + section, number] * SIDE
            total[pl.ds(pl.multiple_of(row, SIDE), SIDE), :] += product


def folded(total, nodes):
    live = pl.ds(0, nodes)
    return total[live, :SIDE] + total[live, SIDE:]


def forward_body(n_in, has_start, choose, first, info, *refs):
    panels, tiles = refs[:n_in], refs[n_in]
    out, split, total, held, sems = refs[-5:]
    nodes, parts = out.shape[0], n_in - int(choose)
    sections = info.shape[0] // 4
    copy, chunks = tile_copies(parts, first, info, tiles, held, sems)
    total[...] = jnp.zeros_like(total)
    for part in range(parts):
        for block in range(nodes // SIDE):
            at = pl.ds(block * SIDE, SIDE)
            value = panels[part][at, :]
            if choose and part == parts - 1:
                value = jnp.where(info[0, CORE] == 0, value, panels[parts][at, :])
            store_split(split, block, value)
        multiply(
            part, info[0, first + part], copy, chunks, info, 1 + sections, 1, False,
            held, split, total,
        )
    value = folded(total, nodes)
    out[...] = value + refs[n_in + 1][...] if has_start else value


def backward_body(parts, first, info, panel, tiles, *refs):
    outs = refs[:parts]
    split, total, held, sems = refs[parts:]
    nodes = panel.shape[0]
    sections = info.shape[0] // 4
    copy, chunks = tile_copies(parts, first, info, tiles, held, sems)
    for block in range(nodes // SIDE):
        store_split(split, block, panel[pl.ds(block * SIDE, SIDE), :])
    for part in range(parts):
        total[...] = jnp.zeros_like(total)
        multiply(
            part, info[0, first + part], copy, chunks, info, 1 + 2 * sections, 1 + 3 * sections,
            True, held, split, total,
        )
        outs[part][...] = folded(total, nodes)


def tile_call(body, parts, info, panels, tiles, extra, n_out, cost):
    slots, (nodes, features) = tiles.shape[1], panels[0].shape
    whole = pl.BlockSpec(memory_space=pltpu.VMEM)
    return pl.pallas_call(
        body,
        in_specs=[pl.BlockSpec(memory_space=pltpu.SMEM)]
        + [whole] * len(panels)
        + [pl.BlockSpec(memory_space=pltpu.HBM)]
        + [whole] * len(extra),
        out_specs=[whole] * n_out,
        scratch_shapes=[
            pltpu.VMEM((nodes // SIDE, 2 * SIDE, 2 * SIDE), BF16),
            pltpu.VMEM((nodes + SIDE, 2 * features), F32),
            pltpu.VMEM((parts, slots, SIDE, SIDE), F32),
            pltpu.SemaphoreType.DMA((parts, slots // CHUNK)),
        ],
        out_shape=[jax.ShapeDtypeStruct((nodes, features), F32)] * n_out,
        compiler_params=pltpu.CompilerParams(vmem_limit_bytes=50 << 20),
        cost_estimate=pl.CostEstimate(
            flops=cost * parts * slots * SIDE * SIDE * features,
            bytes_accessed=4 * parts * slots * SIDE * SIDE,
            transcendentals=0,
        ),
    )(info, *panels, tiles, *extra)


def forward_tiles(first, info, panels, tiles, start, choose):
    extra = [] if start is None else [start]
    body = functools.partial(forward_body, len(panels), start is not None, choose, first)
    return tile_call(body, len(panels) - int(choose), info, panels, tiles, extra, 1, 32)[0]


def backward_tiles(first, info, panel, tiles, parts, cost=32):
    body = functools.partial(backward_body, parts, first)
    return tile_call(body, parts, info, [panel], tiles, [], parts, cost)


def dense_body(partials, weight, cotangent, hidden, spread):
    propagated = partials[0]
    for index in range(1, partials.shape[0]):
        propagated = propagated + partials[index]
    preact = jnp.dot(propagated, weight[...], precision=HIGHEST, preferred_element_type=F32)
    gate = 1.0 / (1.0 + jnp.exp(-preact))
    hidden[...] = preact * gate
    grad_pre = cotangent[...] * gate * (1.0 + preact * (1.0 - gate))
    grad = lax.dot_general(
        grad_pre, weight[...], (((1,), (1,)), ((), ())),
        precision=HIGHEST, preferred_element_type=F32,
    )
    for index in range(spread.shape[0]):
        spread[index] = grad


def dense(partials, weight, cotangent):
    return pl.pallas_call(
        dense_body,
        out_shape=[
            jax.ShapeDtypeStruct(cotangent.shape, F32),
            jax.ShapeDtypeStruct(partials.shape, F32),
        ],
        in_specs=[pl.BlockSpec(memory_space=pltpu.VMEM)] * 3,
        out_specs=[pl.BlockSpec(memory_space=pltpu.VMEM)] * 2,
    )(partials, weight, cotangent)


def shards(features, weight, cotangent, tile_vals, tile_rows, tile_cols, tile_count):
    replicas, groups = lax.axis_size("rep"), lax.axis_size("blk")
    sections = groups // replicas
    rep = lax.axis_index("rep")
    core = lax.axis_index("blk") % 2
    tiles, rows, cols, count = tile_vals[0, 0], tile_rows[0, 0], tile_cols[0, 0], tile_count[0, 0]
    slots = rows.shape[-1]
    live = lax.broadcasted_iota(jnp.int32, rows.shape, 1) < count[:, None]
    lane = lax.broadcasted_iota(jnp.int32, (1, slots), 1)
    plan = jnp.where(lane == 0, 2, 0)
    plan = jnp.where(lane == 1, 3 - 2 * core, plan)
    plan = jnp.where(lane == 3, 1 + 2 * core, plan)
    plan = jnp.where(lane == CORE, core, plan)
    spare = replicas
    info = jnp.concatenate(
        [
            plan,
            jnp.where(live, rows, spare),
            cols ^ rep ^ (rep >> 2),
            rows,
            jnp.where(live, cols ^ rep ^ ((cols ^ rep) >> 2), spare),
        ]
    )

    def device(group, replica):
        return replica * groups + group % groups

    def joint(block, source):
        return lax.ppermute(
            block, ("rep", "blk"),
            [(device(*source(g, r)), device(g, r)) for r in range(replicas) for g in range(groups)],
        )

    def back(block, target):
        return lax.ppermute(
            block, ("rep", "blk"),
            [(device(g, r), device(*target(g, r))) for r in range(replicas) for g in range(groups)],
        )

    def along(block, distance, ids):
        return lax.ppermute(block, "blk", [(g, (g + distance) % groups) for g in ids])

    everyone, evens, odds = range(groups), range(0, groups, 2), range(1, groups, 2)
    twin = [(r ^ 1, r) for r in range(replicas)]
    swap = [(g ^ 1, g) for g in range(groups)]

    own = features[0]
    nodes = own.shape[0]
    pair = lax.dynamic_update_slice(
        jnp.concatenate([own, own]), lax.ppermute(own, "rep", twin), (nodes, 0)
    )
    pair, info = lax.optimization_barrier((pair, info))
    base = jnp.concatenate(
        [
            joint(pair, lambda g, r, k=k: (g + sections * r + 2, r ^ (r >> 2) ^ (2 * k)))
            for k in range(replicas // 2)
        ]
    )
    lower = along(base, 2, everyone)
    upper = along(base, -1, evens)
    beside = lax.ppermute(base, "blk", swap)
    partial_sum = forward_tiles(NEAR, info, [base, beside], tiles, None, False)
    lower, partial_sum = lax.optimization_barrier((lower, partial_sum))
    lower_beside = along(lower, -1, odds)
    partial_sum = forward_tiles(FAR, info, [lower], tiles, partial_sum, False)
    partial_sum = forward_tiles(
        OUTER, info, [lower_beside, upper], tiles, partial_sum, True
    )
    partials = lax.all_to_all(
        partial_sum.reshape(replicas, -1, own.shape[-1]), "rep", 0, 0, tiled=True
    )
    hidden, spread = dense(partials, weight, cotangent[0])
    grad_panel = lax.all_to_all(spread, "rep", 0, 0, tiled=True).reshape(base.shape)
    (outer,) = backward_tiles(OUTER, info, grad_panel, tiles, 1)
    outer_in = along(outer, 1, evens)
    to_lower = along(outer, 1, odds)
    (lowest,) = backward_tiles(LOWEST, info, grad_panel, tiles, 1)
    combined = lowest + outer_in
    from_upper = along(combined, -2, everyone)
    late_panel, _ = lax.optimization_barrier((grad_panel, combined))
    (other,) = backward_tiles(NEAR + 1, info, late_panel, tiles, 1)
    late_panel, other = lax.optimization_barrier((late_panel, other))
    (mine,) = backward_tiles(NEAR, info, late_panel, tiles, 1)
    received = lax.optimization_barrier(mine + from_upper + to_lower)
    total = received + lax.ppermute(other, "blk", swap)
    parts = total.reshape(replicas // 2, -1, own.shape[-1])
    pair_sum = 0.0
    for k in range(replicas // 2):
        part, across = parts[k], (2 * k) ^ (k >> 1)
        if k:
            part = lax.ppermute(part, "rep", [(r, r ^ across) for r in range(replicas)])
        pair_sum = pair_sum + back(
            part, lambda g, r, across=across: (g + sections * (r ^ across) + 2, r)
        )
    kept, sent = jnp.split(pair_sum, 2)
    feature_grad = kept + lax.ppermute(sent, "rep", twin)
    return hidden[None], feature_grad[None]


def solution(mesh):
    placed = (
        P("blk", "rep", None),
        P(),
        P("blk", "rep", None),
        P("blk", "rep", None, None, None, None),
        P("blk", "rep", None, None),
        P("blk", "rep", None, None),
        P("blk", "rep", None),
    )
    return jax.shard_map(
        shards,
        mesh=mesh,
        in_specs=placed,
        out_specs=(P("blk", "rep", None), P("blk", "rep", None)),
        check_vma=False,
    )
```

```python
import functools

import jax
import jax.numpy as jnp
from jax import lax
from jax.experimental import pallas as pl
from jax.experimental.pallas import tpu as pltpu
from jax.sharding import PartitionSpec as P

F32 = jnp.float32
BF16 = jnp.bfloat16
HIGHEST = lax.Precision.HIGHEST
SIDE = 128
CHUNK = 16
NEAR, FAR, OUTER, LOWEST, CORE = 0, 2, 3, 2, 4


def halves(value):
    high = value.astype(BF16)
    return high, (value - high.astype(F32)).astype(BF16)


def store_split(split, block, value):
    high, low = halves(value)
    split[block, :SIDE, :SIDE] = high
    split[block, SIDE:, :SIDE] = high
    split[block, :SIDE, SIDE:] = low
    split[block, SIDE:, SIDE:] = low


def tile_copies(parts, first, info, tiles, held, sems):
    chunks = held.shape[1] // CHUNK

    def copy(part, chunk):
        at = pl.ds(pl.multiple_of(chunk * CHUNK, CHUNK), CHUNK)
        return pltpu.make_async_copy(
            tiles.at[info[0, first + part], at], held.at[part, at], sems.at[part, chunk]
        )

    for part in range(parts):
        for chunk in range(chunks):
            copy(part, chunk).start()
    return copy, chunks


def multiply(part, section, copy, chunks, info, source, target, transposed, held, split, total):
    @pl.loop(0, chunks)
    def _(chunk):
        copy(part, chunk).wait()
        for slot in range(CHUNK):
            number = chunk * CHUNK + slot
            tile = held[part, number]
            left = jnp.concatenate(halves(tile.T if transposed else tile), axis=1)
            right = split[info[source + section, number]]
            product = jnp.dot(left, right, preferred_element_type=F32)
            row = info[target + section, number] * SIDE
            total[pl.ds(pl.multiple_of(row, SIDE), SIDE), :] += product


def folded(total, nodes):
    live = pl.ds(0, nodes)
    return total[live, :SIDE] + total[live, SIDE:]


def forward_body(n_in, has_start, choose, first, info, *refs):
    panels, tiles = refs[:n_in], refs[n_in]
    out, split, total, held, sems = refs[-5:]
    nodes, parts = out.shape[0], n_in - int(choose)
    sections = info.shape[0] // 4
    copy, chunks = tile_copies(parts, first, info, tiles, held, sems)
    total[...] = jnp.zeros_like(total)
    for part in range(parts):
        for block in range(nodes // SIDE):
            at = pl.ds(block * SIDE, SIDE)
            value = panels[part][at, :]
            if choose and part == parts - 1:
                value = jnp.where(info[0, CORE] == 0, value, panels[parts][at, :])
            store_split(split, block, value)
        multiply(
            part, info[0, first + part], copy, chunks, info, 1 + sections, 1, False,
            held, split, total,
        )
    value = folded(total, nodes)
    out[...] = value + refs[n_in + 1][...] if has_start else value


def backward_body(parts, first, info, panel, tiles, *refs):
    outs = refs[:parts]
    split, total, held, sems = refs[parts:]
    nodes = panel.shape[0]
    sections = info.shape[0] // 4
    copy, chunks = tile_copies(parts, first, info, tiles, held, sems)
    for block in range(nodes // SIDE):
        store_split(split, block, panel[pl.ds(block * SIDE, SIDE), :])
    for part in range(parts):
        total[...] = jnp.zeros_like(total)
        multiply(
            part, info[0, first + part], copy, chunks, info, 1 + 2 * sections, 1 + 3 * sections,
            True, held, split, total,
        )
        outs[part][...] = folded(total, nodes)


def tile_call(body, parts, info, panels, tiles, extra, n_out, cost):
    slots, (nodes, features) = tiles.shape[1], panels[0].shape
    whole = pl.BlockSpec(memory_space=pltpu.VMEM)
    return pl.pallas_call(
        body,
        in_specs=[pl.BlockSpec(memory_space=pltpu.SMEM)]
        + [whole] * len(panels)
        + [pl.BlockSpec(memory_space=pltpu.HBM)]
        + [whole] * len(extra),
        out_specs=[whole] * n_out,
        scratch_shapes=[
            pltpu.VMEM((nodes // SIDE, 2 * SIDE, 2 * SIDE), BF16),
            pltpu.VMEM((nodes + SIDE, 2 * features), F32),
            pltpu.VMEM((parts, slots, SIDE, SIDE), F32),
            pltpu.SemaphoreType.DMA((parts, slots // CHUNK)),
        ],
        out_shape=[jax.ShapeDtypeStruct((nodes, features), F32)] * n_out,
        compiler_params=pltpu.CompilerParams(vmem_limit_bytes=50 << 20),
        cost_estimate=pl.CostEstimate(
            flops=cost * parts * slots * SIDE * SIDE * features,
            bytes_accessed=4 * parts * slots * SIDE * SIDE,
            transcendentals=0,
        ),
    )(info, *panels, tiles, *extra)


def forward_tiles(first, info, panels, tiles, start, choose):
    extra = [] if start is None else [start]
    body = functools.partial(forward_body, len(panels), start is not None, choose, first)
    return tile_call(body, len(panels) - int(choose), info, panels, tiles, extra, 1, 32)[0]


def backward_tiles(first, info, panel, tiles, parts, cost=32):
    body = functools.partial(backward_body, parts, first)
    return tile_call(body, parts, info, [panel], tiles, [], parts, cost)


def dense_body(partials, weight, cotangent, hidden, spread):
    propagated = partials[0]
    for index in range(1, partials.shape[0]):
        propagated = propagated + partials[index]
    preact = jnp.dot(propagated, weight[...], precision=HIGHEST, preferred_element_type=F32)
    gate = 1.0 / (1.0 + jnp.exp(-preact))
    hidden[...] = preact * gate
    grad_pre = cotangent[...] * gate * (1.0 + preact * (1.0 - gate))
    grad = lax.dot_general(
        grad_pre, weight[...], (((1,), (1,)), ((), ())),
        precision=HIGHEST, preferred_element_type=F32,
    )
    for index in range(spread.shape[0]):
        spread[index] = grad


def dense(partials, weight, cotangent):
    return pl.pallas_call(
        dense_body,
        out_shape=[
            jax.ShapeDtypeStruct(cotangent.shape, F32),
            jax.ShapeDtypeStruct(partials.shape, F32),
        ],
        in_specs=[pl.BlockSpec(memory_space=pltpu.VMEM)] * 3,
        out_specs=[pl.BlockSpec(memory_space=pltpu.VMEM)] * 2,
    )(partials, weight, cotangent)


def shards(features, weight, cotangent, tile_vals, tile_rows, tile_cols, tile_count):
    replicas, groups = lax.axis_size("rep"), lax.axis_size("blk")
    sections = groups // replicas
    rep = lax.axis_index("rep")
    group = lax.axis_index("blk")
    core = group % 2
    tiles, rows, cols, count = tile_vals[0, 0], tile_rows[0, 0], tile_cols[0, 0], tile_count[0, 0]
    slots = rows.shape[-1]
    live = lax.broadcasted_iota(jnp.int32, rows.shape, 1) < count[:, None]
    lane = lax.broadcasted_iota(jnp.int32, (1, slots), 1)
    plan = jnp.where(lane == 0, 2, 0)
    plan = jnp.where(lane == 1, 3 - 2 * core, plan)
    plan = jnp.where(lane == 3, 1 + 2 * core, plan)
    plan = jnp.where(lane == CORE, core, plan)
    spare = replicas
    span, half = groups // 2, replicas // 2
    step = lax.broadcasted_iota(jnp.int32, cols.shape, 0)
    turned = jnp.where((group % span < 2) & (step == 1 - core), half | (half >> 2), 0)
    source = cols ^ rep
    target = source ^ (source >> 2) ^ turned
    info = jnp.concatenate(
        [
            plan,
            jnp.where(live, rows, spare),
            source ^ (rep >> 2) ^ turned,
            rows,
            jnp.where(live, target, spare),
        ]
    )

    def device(group, replica):
        return replica * groups + group % groups

    def joint(block, source):
        return lax.ppermute(
            block, ("rep", "blk"),
            [(device(*source(g, r)), device(g, r)) for r in range(replicas) for g in range(groups)],
        )

    def back(block, target):
        return lax.ppermute(
            block, ("rep", "blk"),
            [(device(g, r), device(*target(g, r))) for r in range(replicas) for g in range(groups)],
        )

    def below(group, replica):
        lower = (group - 2) % groups
        if group % span < 2 and group % 2:
            return lower ^ span, replica ^ half
        return lower, replica

    def along(block, distance, ids):
        return lax.ppermute(block, "blk", [(g, (g + distance) % groups) for g in ids])

    evens, odds = range(0, groups, 2), range(1, groups, 2)
    twin = [(r ^ 1, r) for r in range(replicas)]
    swap = [(g ^ 1, g) for g in range(groups)]

    own = features[0]
    nodes = own.shape[0]
    pair = lax.dynamic_update_slice(
        jnp.concatenate([own, own]), lax.ppermute(own, "rep", twin), (nodes, 0)
    )
    pair, info = lax.optimization_barrier((pair, info))
    base = jnp.concatenate(
        [
            joint(pair, lambda g, r, k=k: (g + sections * r + 2, r ^ (r >> 2) ^ (2 * k)))
            for k in range(replicas // 2)
        ]
    )
    lower = joint(base, below)
    upper = along(base, -1, evens)
    beside = lax.ppermute(base, "blk", swap)
    partial_sum = forward_tiles(NEAR, info, [base, beside], tiles, None, False)
    lower, partial_sum = lax.optimization_barrier((lower, partial_sum))
    lower_beside = along(lower, -1, odds)
    partial_sum = forward_tiles(FAR, info, [lower], tiles, partial_sum, False)
    partial_sum = forward_tiles(
        OUTER, info, [lower_beside, upper], tiles, partial_sum, True
    )
    partials = lax.all_to_all(
        partial_sum.reshape(replicas, -1, own.shape[-1]), "rep", 0, 0, tiled=True
    )
    hidden, spread = dense(partials, weight, cotangent[0])
    grad_panel = lax.all_to_all(spread, "rep", 0, 0, tiled=True).reshape(base.shape)
    (outer,) = backward_tiles(OUTER, info, grad_panel, tiles, 1)
    outer_in = along(outer, 1, evens)
    to_lower = along(outer, 1, odds)
    (lowest,) = backward_tiles(LOWEST, info, grad_panel, tiles, 1)
    combined = lowest + outer_in
    from_upper = back(combined, below)
    late_panel, _ = lax.optimization_barrier((grad_panel, combined))
    (other,) = backward_tiles(NEAR + 1, info, late_panel, tiles, 1)
    late_panel, other = lax.optimization_barrier((late_panel, other))
    (mine,) = backward_tiles(NEAR, info, late_panel, tiles, 1)
    received = lax.optimization_barrier(mine + from_upper + to_lower)
    total = received + lax.ppermute(other, "blk", swap)
    parts = total.reshape(replicas // 2, -1, own.shape[-1])
    pair_sum = 0.0
    for k in range(replicas // 2):
        part, across = parts[k], (2 * k) ^ (k >> 1)
        if k:
            part = lax.ppermute(part, "rep", [(r, r ^ across) for r in range(replicas)])
        pair_sum = pair_sum + back(
            part, lambda g, r, across=across: (g + sections * (r ^ across) + 2, r)
        )
    kept, sent = jnp.split(pair_sum, 2)
    feature_grad = kept + lax.ppermute(sent, "rep", twin)
    return hidden[None], feature_grad[None]


def solution(mesh):
    placed = (
        P("blk", "rep", None),
        P(),
        P("blk", "rep", None),
        P("blk", "rep", None, None, None, None),
        P("blk", "rep", None, None),
        P("blk", "rep", None, None),
        P("blk", "rep", None),
    )
    return jax.shard_map(
        shards,
        mesh=mesh,
        in_specs=placed,
        out_specs=(P("blk", "rep", None), P("blk", "rep", None)),
        check_vma=False,
    )
```

```python
import functools

import jax
import jax.numpy as jnp
from jax import lax
from jax.experimental import pallas as pl
from jax.experimental.pallas import tpu as pltpu
from jax.sharding import PartitionSpec as P

F32 = jnp.float32
BF16 = jnp.bfloat16
SIDE = 128
CHUNK = 16
LIMIT = 48
NEAR, FAR, OUTER, LOWEST, CORE = 0, 2, 3, 2, 4


def halves(value):
    high = value.astype(BF16)
    return high, (value - high.astype(F32)).astype(BF16)


def store_split(split, block, value):
    high, low = halves(value)
    split[block, :SIDE, :SIDE] = high
    split[block, SIDE:, :SIDE] = high
    split[block, :SIDE, SIDE:] = low
    split[block, SIDE:, SIDE:] = low


def tile_copies(parts, first, info, tiles, held, sems):
    chunks = held.shape[1] // CHUNK

    def copy(part, chunk):
        at = pl.ds(pl.multiple_of(chunk * CHUNK, CHUNK), CHUNK)
        return pltpu.make_async_copy(
            tiles.at[info[0, first + part], at], held.at[part, at], sems.at[part, chunk]
        )

    for part in range(parts):
        for chunk in range(chunks):
            copy(part, chunk).start()
    return copy, chunks


def multiply(left_of, part, section, chunks, info, source, target, split, total):
    @pl.loop(0, chunks)
    def _(chunk):
        for left, number in left_of(part, chunk):
            right = split[info[source + section, number]]
            product = jnp.dot(left, right, preferred_element_type=F32)
            row = info[target + section, number] * SIDE
            total[pl.ds(pl.multiple_of(row, SIDE), SIDE), :] += product


def fetched(parts, first, info, tiles, held, sems, transposed):
    copy, chunks = tile_copies(parts, first, info, tiles, held, sems)

    def left_of(part, chunk):
        copy(part, chunk).wait()
        for slot in range(CHUNK):
            number = chunk * CHUNK + slot
            tile = held[part, number]
            yield jnp.concatenate(halves(tile.T if transposed else tile), axis=1), number

    return left_of, chunks


def prepared(tiles):
    def left_of(part, chunk):
        for slot in range(CHUNK):
            number = chunk * CHUNK + slot
            yield tiles[number], number

    return left_of, tiles.shape[0] // CHUNK


def folded(total, nodes):
    live = pl.ds(0, nodes)
    return total[live, :SIDE] + total[live, SIDE:]


def prepare_body(parts, first, transposed, info, tiles, *refs):
    outs, (held, sems) = refs[:parts], refs[parts:]
    left_of, chunks = fetched(parts, first, info, tiles, held, sems, transposed)
    for part in range(parts):

        @pl.loop(0, chunks)
        def _(chunk, part=part):
            for left, number in left_of(part, chunk):
                outs[part][number] = left


def forward_body(n_in, has_start, choose, first, info, *refs):
    panels, tiles = refs[:n_in], refs[n_in]
    out, split, total = refs[n_in + 1 + int(has_start) :][:3]
    nodes, parts = out.shape[0], n_in - int(choose)
    sections = info.shape[0] // 4
    if tiles.dtype == F32:
        left_of, chunks = fetched(parts, first, info, tiles, *refs[-2:], False)
    else:
        left_of, chunks = prepared(tiles)
    total[...] = jnp.zeros_like(total)
    for part in range(parts):
        for block in range(nodes // SIDE):
            at = pl.ds(block * SIDE, SIDE)
            value = panels[part][at, :]
            if choose and part == parts - 1:
                value = jnp.where(info[0, CORE] == 0, value, panels[parts][at, :])
            store_split(split, block, value)
        multiply(
            left_of, part, info[0, first + part], chunks, info, 1 + sections, 1, split, total
        )
    value = folded(total, nodes)
    out[...] = value + refs[n_in + 1][...] if has_start else value


def backward_body(parts, first, info, panel, tiles, *refs):
    outs = refs[:parts]
    split, total = refs[parts : parts + 2]
    nodes = panel.shape[0]
    sections = info.shape[0] // 4
    if tiles.dtype == F32:
        left_of, chunks = fetched(parts, first, info, tiles, *refs[-2:], True)
    else:
        left_of, chunks = prepared(tiles)
    for block in range(nodes // SIDE):
        store_split(split, block, panel[pl.ds(block * SIDE, SIDE), :])
    for part in range(parts):
        total[...] = jnp.zeros_like(total)
        multiply(
            left_of, part, info[0, first + part], chunks, info, 1 + 2 * sections,
            1 + 3 * sections, split, total,
        )
        outs[part][...] = folded(total, nodes)


def local_call(body, parts, slots, info, panels, tiles, extra, outs, scratch):
    whole = pl.BlockSpec(memory_space=pltpu.VMEM)
    raw = tiles.dtype == F32
    if raw:
        scratch = scratch + [
            pltpu.VMEM((parts, slots, SIDE, SIDE), F32),
            pltpu.SemaphoreType.DMA((parts, slots // CHUNK)),
        ]
    return pl.pallas_call(
        body,
        in_specs=[pl.BlockSpec(memory_space=pltpu.SMEM)]
        + [whole] * len(panels)
        + [pl.BlockSpec(memory_space=pltpu.HBM) if raw else whole]
        + [whole] * len(extra),
        out_specs=[whole] * len(outs),
        scratch_shapes=scratch,
        out_shape=outs,
        compiler_params=pltpu.CompilerParams(vmem_limit_bytes=LIMIT << 20),
        cost_estimate=pl.CostEstimate(
            flops=32 * parts * slots * SIDE**3,
            bytes_accessed=4 * parts * slots * SIDE * SIDE,
            transcendentals=0,
        ),
    )(info, *panels, tiles, *extra)


def tile_call(body, parts, info, panels, tiles, extra, n_out):
    nodes, features = panels[0].shape
    return local_call(
        body, parts, tiles.shape[-3], info, panels, tiles, extra,
        [jax.ShapeDtypeStruct((nodes, features), F32)] * n_out,
        [
            pltpu.VMEM((nodes // SIDE, 2 * SIDE, 2 * SIDE), BF16),
            pltpu.VMEM((nodes + SIDE, 2 * features), F32),
        ],
    )


def prepare(parts, first, transposed, info, tiles):
    slots = tiles.shape[1]
    body = functools.partial(prepare_body, parts, first, transposed)
    shape = jax.ShapeDtypeStruct((slots, SIDE, 2 * SIDE), BF16)
    return local_call(body, parts, slots, info, [], tiles, [], [shape] * parts, [])


def forward_tiles(first, info, panels, tiles, start, choose):
    extra = [] if start is None else [start]
    body = functools.partial(forward_body, len(panels), start is not None, choose, first)
    return tile_call(body, len(panels) - int(choose), info, panels, tiles, extra, 1)[0]


def backward_tiles(first, info, panel, tiles, parts):
    body = functools.partial(backward_body, parts, first)
    return tile_call(body, parts, info, [panel], tiles, [], parts)


def widened(value):
    both = jnp.concatenate(halves(value), axis=1)
    return jnp.concatenate([both, both], axis=0)


def split_dot(left, right):
    wide = jnp.dot(
        jnp.concatenate(halves(left), axis=1), widened(right), preferred_element_type=F32
    )
    middle = right.shape[1]
    return wide[:, :middle] + wide[:, middle:]


def dense_body(partials, weight, cotangent, hidden, spread):
    propagated = partials[0]
    for index in range(1, partials.shape[0]):
        propagated = propagated + partials[index]
    preact = split_dot(propagated, weight[...])
    gate = 1.0 / (1.0 + jnp.exp(-preact))
    hidden[...] = preact * gate
    grad_pre = cotangent[...] * gate * (1.0 + preact * (1.0 - gate))
    grad = split_dot(grad_pre, weight[...].T)
    for index in range(spread.shape[0]):
        spread[index] = grad


def dense(partials, weight, cotangent):
    return pl.pallas_call(
        dense_body,
        out_shape=[
            jax.ShapeDtypeStruct(cotangent.shape, F32),
            jax.ShapeDtypeStruct(partials.shape, F32),
        ],
        in_specs=[pl.BlockSpec(memory_space=pltpu.VMEM)] * 3,
        out_specs=[pl.BlockSpec(memory_space=pltpu.VMEM)] * 2,
    )(partials, weight, cotangent)


def shards(features, weight, cotangent, tile_vals, tile_rows, tile_cols, tile_count):
    replicas, groups = lax.axis_size("rep"), lax.axis_size("blk")
    sections = groups // replicas
    rep = lax.axis_index("rep")
    group = lax.axis_index("blk")
    core = group % 2
    tiles, rows, cols, count = tile_vals[0, 0], tile_rows[0, 0], tile_cols[0, 0], tile_count[0, 0]
    slots = rows.shape[-1]
    live = lax.broadcasted_iota(jnp.int32, rows.shape, 1) < count[:, None]
    lane = lax.broadcasted_iota(jnp.int32, (1, slots), 1)
    plan = jnp.where(lane == 0, 2, 0)
    plan = jnp.where(lane == 1, 3 - 2 * core, plan)
    plan = jnp.where(lane == 3, 1 + 2 * core, plan)
    plan = jnp.where(lane == CORE, core, plan)
    spare = replicas
    span, half = groups // 2, replicas // 2
    step = lax.broadcasted_iota(jnp.int32, cols.shape, 0)
    turned = jnp.where((group % span < 2) & (step == 1 - core), half | (half >> 2), 0)
    source = cols ^ rep
    target = source ^ (source >> 2) ^ turned
    info = jnp.concatenate(
        [
            plan,
            jnp.where(live, rows, spare),
            source ^ (rep >> 2) ^ turned,
            rows,
            jnp.where(live, target, spare),
        ]
    )

    def device(group, replica):
        return replica * groups + group % groups

    def joint(block, source):
        return lax.ppermute(
            block, ("rep", "blk"),
            [(device(*source(g, r)), device(g, r)) for r in range(replicas) for g in range(groups)],
        )

    def back(block, target):
        return lax.ppermute(
            block, ("rep", "blk"),
            [(device(g, r), device(*target(g, r))) for r in range(replicas) for g in range(groups)],
        )

    def below(group, replica):
        lower = (group - 2) % groups
        if group % span < 2 and group % 2:
            return lower ^ span, replica ^ half
        return lower, replica

    def along(block, distance, ids):
        return lax.ppermute(block, "blk", [(g, (g + distance) % groups) for g in ids])

    evens, odds = range(0, groups, 2), range(1, groups, 2)
    twin = [(r ^ 1, r) for r in range(replicas)]
    swap = [(g ^ 1, g) for g in range(groups)]

    own = features[0]
    nodes = own.shape[0]
    pair = lax.dynamic_update_slice(
        jnp.concatenate([own, own]), lax.ppermute(own, "rep", twin), (nodes, 0)
    )
    pair, info = lax.optimization_barrier((pair, info))
    low_tiles, rest_tiles = prepare(2, FAR, False, info, tiles)
    base = jnp.concatenate(
        [
            joint(pair, lambda g, r, k=k: (g + sections * r + 2, r ^ (r >> 2) ^ (2 * k)))
            for k in range(replicas // 2)
        ]
    )
    base, low_tiles, rest_tiles = lax.optimization_barrier((base, low_tiles, rest_tiles))
    lower = joint(base, below)
    upper = along(base, -1, evens)
    beside = lax.ppermute(base, "blk", swap)
    partial_sum = forward_tiles(NEAR, info, [base, beside], tiles, None, False)
    lower, partial_sum = lax.optimization_barrier((lower, partial_sum))
    lower_beside = along(lower, -1, odds)
    partial_sum = forward_tiles(FAR, info, [lower], low_tiles, partial_sum, False)
    partial_sum = forward_tiles(
        OUTER, info, [lower_beside, upper], rest_tiles, partial_sum, True
    )
    late_info, partial_sum = lax.optimization_barrier((info, partial_sum))
    (outer_tiles,) = prepare(1, OUTER, True, late_info, tiles)
    partials = lax.all_to_all(
        partial_sum.reshape(replicas, -1, own.shape[-1]), "rep", 0, 0, tiled=True
    )
    hidden, spread = dense(partials, weight, cotangent[0])
    grad_panel = lax.all_to_all(spread, "rep", 0, 0, tiled=True).reshape(base.shape)
    (outer,) = backward_tiles(OUTER, info, grad_panel, outer_tiles, 1)
    outer_in = along(outer, 1, evens)
    to_lower = along(outer, 1, odds)
    (lowest,) = backward_tiles(LOWEST, info, grad_panel, tiles, 1)
    combined = lowest + outer_in
    from_upper = back(combined, below)
    late_panel, _ = lax.optimization_barrier((grad_panel, combined))
    (other,) = backward_tiles(NEAR + 1, info, late_panel, tiles, 1)
    late_panel, other = lax.optimization_barrier((late_panel, other))
    (mine,) = backward_tiles(NEAR, info, late_panel, tiles, 1)
    received = lax.optimization_barrier(mine + from_upper + to_lower)
    total = received + lax.ppermute(other, "blk", swap)
    parts = total.reshape(replicas // 2, -1, own.shape[-1])
    pair_sum = 0.0
    for k in range(replicas // 2):
        part, across = parts[k], (2 * k) ^ (k >> 1)
        if k:
            part = lax.ppermute(part, "rep", [(r, r ^ across) for r in range(replicas)])
        pair_sum = pair_sum + back(
            part, lambda g, r, across=across: (g + sections * (r ^ across) + 2, r)
        )
    kept, sent = jnp.split(pair_sum, 2)
    feature_grad = kept + lax.ppermute(sent, "rep", twin)
    return hidden[None], feature_grad[None]


def solution(mesh):
    placed = (
        P("blk", "rep", None),
        P(),
        P("blk", "rep", None),
        P("blk", "rep", None, None, None, None),
        P("blk", "rep", None, None),
        P("blk", "rep", None, None),
        P("blk", "rep", None),
    )
    return jax.shard_map(
        shards,
        mesh=mesh,
        in_specs=placed,
        out_specs=(P("blk", "rep", None), P("blk", "rep", None)),
        check_vma=False,
    )
```

```python
import functools

import jax
import jax.numpy as jnp
from jax import lax
from jax.experimental import pallas as pl
from jax.experimental.pallas import tpu as pltpu
from jax.sharding import PartitionSpec as P

F32 = jnp.float32
BF16 = jnp.bfloat16
SIDE = 128
CHUNK = 16
LIMIT, DENSE_LIMIT = 48, 16
NEAR, FAR, OUTER, LOWEST, CORE = 0, 2, 3, 2, 4


def halves(value):
    high = value.astype(BF16)
    return high, (value - high.astype(F32)).astype(BF16)


def store_split(split, block, value):
    high, low = halves(value)
    split[block, :SIDE, :SIDE] = high
    split[block, SIDE:, :SIDE] = high
    split[block, :SIDE, SIDE:] = low
    split[block, SIDE:, SIDE:] = low


def tile_copies(parts, first, info, tiles, held, sems):
    chunks = held.shape[1] // CHUNK

    def copy(part, chunk):
        at = pl.ds(pl.multiple_of(chunk * CHUNK, CHUNK), CHUNK)
        return pltpu.make_async_copy(
            tiles.at[info[0, first + part], at], held.at[part, at], sems.at[part, chunk]
        )

    for part in range(parts):
        for chunk in range(chunks):
            copy(part, chunk).start()
    return copy, chunks


def multiply(left_of, part, section, chunks, info, source, target, split, total):
    @pl.loop(0, chunks)
    def _(chunk):
        for left, number in left_of(part, chunk):
            right = split[info[source + section, number]]
            product = jnp.dot(left, right, preferred_element_type=F32)
            row = info[target + section, number] * SIDE
            total[pl.ds(pl.multiple_of(row, SIDE), SIDE), :] += product


def fetched(parts, first, info, tiles, held, sems, transposed):
    copy, chunks = tile_copies(parts, first, info, tiles, held, sems)

    def left_of(part, chunk):
        copy(part, chunk).wait()
        for slot in range(CHUNK):
            number = chunk * CHUNK + slot
            tile = held[part, number]
            yield jnp.concatenate(halves(tile.T if transposed else tile), axis=1), number

    return left_of, chunks


def prepared(tiles):
    def left_of(part, chunk):
        for slot in range(CHUNK):
            number = chunk * CHUNK + slot
            yield tiles[number], number

    return left_of, tiles.shape[0] // CHUNK


def folded(total, nodes):
    live = pl.ds(0, nodes)
    return total[live, :SIDE] + total[live, SIDE:]


def prepare_body(parts, first, transposed, info, tiles, *refs):
    outs, (held, sems) = refs[:parts], refs[parts:]
    left_of, chunks = fetched(parts, first, info, tiles, held, sems, transposed)
    for part in range(parts):

        @pl.loop(0, chunks)
        def _(chunk, part=part):
            for left, number in left_of(part, chunk):
                outs[part][number] = left


def forward_body(n_in, has_start, choose, first, info, *refs):
    panels, tiles = refs[:n_in], refs[n_in]
    out, split, total = refs[n_in + 1 + int(has_start) :][:3]
    nodes, parts = out.shape[0], n_in - int(choose)
    sections = info.shape[0] // 4
    if tiles.dtype == F32:
        left_of, chunks = fetched(parts, first, info, tiles, *refs[-2:], False)
    else:
        left_of, chunks = prepared(tiles)
    total[...] = jnp.zeros_like(total)
    for part in range(parts):
        for block in range(nodes // SIDE):
            at = pl.ds(block * SIDE, SIDE)
            value = panels[part][at, :]
            if choose and part == parts - 1:
                value = jnp.where(info[0, CORE] == 0, value, panels[parts][at, :])
            store_split(split, block, value)
        multiply(
            left_of, part, info[0, first + part], chunks, info, 1 + sections, 1, split, total
        )
    value = folded(total, nodes)
    out[...] = value + refs[n_in + 1][...] if has_start else value


def backward_body(parts, first, info, panel, tiles, *refs):
    outs = refs[:parts]
    split, total = refs[parts : parts + 2]
    nodes = panel.shape[0]
    sections = info.shape[0] // 4
    if tiles.dtype == F32:
        left_of, chunks = fetched(parts, first, info, tiles, *refs[-2:], True)
    else:
        left_of, chunks = prepared(tiles)
    for block in range(nodes // SIDE):
        store_split(split, block, panel[pl.ds(block * SIDE, SIDE), :])
    for part in range(parts):
        total[...] = jnp.zeros_like(total)
        multiply(
            left_of, part, info[0, first + part], chunks, info, 1 + 2 * sections,
            1 + 3 * sections, split, total,
        )
        outs[part][...] = folded(total, nodes)


def local_call(body, parts, slots, info, panels, tiles, extra, outs, scratch):
    whole = pl.BlockSpec(memory_space=pltpu.VMEM)
    raw = tiles.dtype == F32
    if raw:
        scratch = scratch + [
            pltpu.VMEM((parts, slots, SIDE, SIDE), F32),
            pltpu.SemaphoreType.DMA((parts, slots // CHUNK)),
        ]
    return pl.pallas_call(
        body,
        in_specs=[pl.BlockSpec(memory_space=pltpu.SMEM)]
        + [whole] * len(panels)
        + [pl.BlockSpec(memory_space=pltpu.HBM) if raw else whole]
        + [whole] * len(extra),
        out_specs=[whole] * len(outs),
        scratch_shapes=scratch,
        out_shape=outs,
        compiler_params=pltpu.CompilerParams(vmem_limit_bytes=LIMIT << 20),
        cost_estimate=pl.CostEstimate(
            flops=32 * parts * slots * SIDE**3,
            bytes_accessed=4 * parts * slots * SIDE * SIDE,
            transcendentals=0,
        ),
    )(info, *panels, tiles, *extra)


def tile_call(body, parts, info, panels, tiles, extra, n_out):
    nodes, features = panels[0].shape
    return local_call(
        body, parts, tiles.shape[-3], info, panels, tiles, extra,
        [jax.ShapeDtypeStruct((nodes, features), F32)] * n_out,
        [
            pltpu.VMEM((nodes // SIDE, 2 * SIDE, 2 * SIDE), BF16),
            pltpu.VMEM((nodes + SIDE, 2 * features), F32),
        ],
    )


def prepare(parts, first, transposed, info, tiles):
    slots = tiles.shape[1]
    body = functools.partial(prepare_body, parts, first, transposed)
    shape = jax.ShapeDtypeStruct((slots, SIDE, 2 * SIDE), BF16)
    return local_call(body, parts, slots, info, [], tiles, [], [shape] * parts, [])


def forward_tiles(first, info, panels, tiles, start, choose):
    extra = [] if start is None else [start]
    body = functools.partial(forward_body, len(panels), start is not None, choose, first)
    return tile_call(body, len(panels) - int(choose), info, panels, tiles, extra, 1)[0]


def backward_tiles(first, info, panel, tiles, parts):
    body = functools.partial(backward_body, parts, first)
    return tile_call(body, parts, info, [panel], tiles, [], parts)


def widened(value):
    both = jnp.concatenate(halves(value), axis=1)
    return jnp.concatenate([both, both], axis=0)


def split_dot(left, right):
    wide = jnp.dot(
        jnp.concatenate(halves(left), axis=1), widened(right), preferred_element_type=F32
    )
    middle = right.shape[1]
    return wide[:, :middle] + wide[:, middle:]


def dense_body(partials, weight, cotangent, hidden, spread):
    propagated = partials[0]
    for index in range(1, partials.shape[0]):
        propagated = propagated + partials[index]
    preact = split_dot(propagated, weight[...])
    gate = 1.0 / (1.0 + jnp.exp(-preact))
    hidden[...] = preact * gate
    grad_pre = cotangent[...] * gate * (1.0 + preact * (1.0 - gate))
    grad = split_dot(grad_pre, weight[...].T)
    for index in range(spread.shape[0]):
        spread[index] = grad


def dense(partials, weight, cotangent):
    return pl.pallas_call(
        dense_body,
        out_shape=[
            jax.ShapeDtypeStruct(cotangent.shape, F32),
            jax.ShapeDtypeStruct(partials.shape, F32),
        ],
        in_specs=[pl.BlockSpec(memory_space=pltpu.VMEM)] * 3,
        out_specs=[pl.BlockSpec(memory_space=pltpu.VMEM)] * 2,
        compiler_params=pltpu.CompilerParams(vmem_limit_bytes=DENSE_LIMIT << 20),
    )(partials, weight, cotangent)


def shards(features, weight, cotangent, tile_vals, tile_rows, tile_cols, tile_count):
    replicas, groups = lax.axis_size("rep"), lax.axis_size("blk")
    sections = groups // replicas
    rep = lax.axis_index("rep")
    group = lax.axis_index("blk")
    core = group % 2
    tiles, rows, cols, count = tile_vals[0, 0], tile_rows[0, 0], tile_cols[0, 0], tile_count[0, 0]
    slots = rows.shape[-1]
    live = lax.broadcasted_iota(jnp.int32, rows.shape, 1) < count[:, None]
    lane = lax.broadcasted_iota(jnp.int32, (1, slots), 1)
    plan = jnp.where(lane == 0, 2, 0)
    plan = jnp.where(lane == 1, 3 - 2 * core, plan)
    plan = jnp.where(lane == 3, 1 + 2 * core, plan)
    plan = jnp.where(lane == CORE, core, plan)
    spare = replicas
    span, half = groups // 2, replicas // 2
    step = lax.broadcasted_iota(jnp.int32, cols.shape, 0)
    turned = jnp.where((group % span < 2) & (step == 1 - core), half | (half >> 2), 0)
    source = cols ^ rep
    target = source ^ (source >> 2) ^ turned
    info = jnp.concatenate(
        [
            plan,
            jnp.where(live, rows, spare),
            source ^ (rep >> 2) ^ turned,
            rows,
            jnp.where(live, target, spare),
        ]
    )

    def device(group, replica):
        return replica * groups + group % groups

    def joint(block, source):
        return lax.ppermute(
            block, ("rep", "blk"),
            [(device(*source(g, r)), device(g, r)) for r in range(replicas) for g in range(groups)],
        )

    def back(block, target):
        return lax.ppermute(
            block, ("rep", "blk"),
            [(device(g, r), device(*target(g, r))) for r in range(replicas) for g in range(groups)],
        )

    def below(group, replica):
        lower = (group - 2) % groups
        if group % span < 2 and group % 2:
            return lower ^ span, replica ^ half
        return lower, replica

    def along(block, distance, ids):
        return lax.ppermute(block, "blk", [(g, (g + distance) % groups) for g in ids])

    evens, odds = range(0, groups, 2), range(1, groups, 2)
    twin = [(r ^ 1, r) for r in range(replicas)]
    swap = [(g ^ 1, g) for g in range(groups)]

    own = features[0]
    nodes = own.shape[0]
    pair = lax.dynamic_update_slice(
        jnp.concatenate([own, own]), lax.ppermute(own, "rep", twin), (nodes, 0)
    )
    pair, info = lax.optimization_barrier((pair, info))
    low_tiles, rest_tiles = prepare(2, FAR, False, info, tiles)
    base = jnp.concatenate(
        [
            joint(pair, lambda g, r, k=k: (g + sections * r + 2, r ^ (r >> 2) ^ (2 * k)))
            for k in range(replicas // 2)
        ]
    )
    base, low_tiles, rest_tiles = lax.optimization_barrier((base, low_tiles, rest_tiles))
    lower = joint(base, below)
    upper = along(base, -1, evens)
    beside = lax.ppermute(base, "blk", swap)
    partial_sum = forward_tiles(NEAR, info, [base, beside], tiles, None, False)
    lower, partial_sum = lax.optimization_barrier((lower, partial_sum))
    lower_beside = along(lower, -1, odds)
    partial_sum = forward_tiles(FAR, info, [lower], low_tiles, partial_sum, False)
    partial_sum = forward_tiles(
        OUTER, info, [lower_beside, upper], rest_tiles, partial_sum, True
    )
    late_info, partial_sum = lax.optimization_barrier((info, partial_sum))
    (outer_tiles,) = prepare(1, OUTER, True, late_info, tiles)
    partials = lax.all_to_all(
        partial_sum.reshape(replicas, -1, own.shape[-1]), "rep", 0, 0, tiled=True
    )
    hidden, spread = dense(partials, weight, cotangent[0])
    grad_panel = lax.all_to_all(spread, "rep", 0, 0, tiled=True).reshape(base.shape)
    (outer,) = backward_tiles(OUTER, info, grad_panel, outer_tiles, 1)
    outer_in = along(outer, 1, evens)
    (lowest,) = backward_tiles(LOWEST, info, grad_panel, tiles, 1)
    combined = lowest + outer_in
    from_upper = back(combined, below)
    outer, combined = lax.optimization_barrier((outer, combined))
    to_lower = along(outer, 1, odds)
    late_panel, _ = lax.optimization_barrier((grad_panel, combined))
    (other,) = backward_tiles(NEAR + 1, info, late_panel, tiles, 1)
    late_panel, other = lax.optimization_barrier((late_panel, other))
    (mine,) = backward_tiles(NEAR, info, late_panel, tiles, 1)
    received = lax.optimization_barrier(mine + from_upper + to_lower)
    total = received + lax.ppermute(other, "blk", swap)
    parts = total.reshape(replicas // 2, -1, own.shape[-1])
    pair_sum = 0.0
    for k in range(replicas // 2):
        part, across = parts[k], (2 * k) ^ (k >> 1)
        if k:
            part = lax.ppermute(part, "rep", [(r, r ^ across) for r in range(replicas)])
        pair_sum = pair_sum + back(
            part, lambda g, r, across=across: (g + sections * (r ^ across) + 2, r)
        )
    kept, sent = jnp.split(pair_sum, 2)
    feature_grad = kept + lax.ppermute(sent, "rep", twin)
    return hidden[None], feature_grad[None]


def solution(mesh):
    placed = (
        P("blk", "rep", None),
        P(),
        P("blk", "rep", None),
        P("blk", "rep", None, None, None, None),
        P("blk", "rep", None, None),
        P("blk", "rep", None, None),
        P("blk", "rep", None),
    )
    return jax.shard_map(
        shards,
        mesh=mesh,
        in_specs=placed,
        out_specs=(P("blk", "rep", None), P("blk", "rep", None)),
        check_vma=False,
    )
```

```python
import functools

import jax
import jax.numpy as jnp
from jax import lax
from jax.experimental import pallas as pl
from jax.experimental.pallas import tpu as pltpu
from jax.sharding import PartitionSpec as P

F32 = jnp.float32
BF16 = jnp.bfloat16
SIDE = 128
CHUNK = 16
LIMIT, DENSE_LIMIT = 48, 16
NEAR, FAR, OUTER, LOWEST, CORE = 0, 2, 3, 2, 4


def halves(value):
    high = value.astype(BF16)
    return high, (value - high.astype(F32)).astype(BF16)


def store_split(split, block, value):
    high, low = halves(value)
    split[block, :SIDE, :SIDE] = high
    split[block, SIDE:, :SIDE] = high
    split[block, :SIDE, SIDE:] = low
    split[block, SIDE:, SIDE:] = low


def tile_copies(parts, first, info, tiles, held, sems):
    chunks = held.shape[1] // CHUNK

    def copy(part, chunk):
        at = pl.ds(pl.multiple_of(chunk * CHUNK, CHUNK), CHUNK)
        return pltpu.make_async_copy(
            tiles.at[info[0, first + part], at], held.at[part, at], sems.at[part, chunk]
        )

    for part in range(parts):
        for chunk in range(chunks):
            copy(part, chunk).start()
    return copy, chunks


def multiply(left_of, part, section, chunks, info, source, target, split, total):
    @pl.loop(0, chunks)
    def _(chunk):
        for left, number in left_of(part, chunk):
            right = split[info[source + section, number]]
            product = jnp.dot(left, right, preferred_element_type=F32)
            row = info[target + section, number] * SIDE
            total[pl.ds(pl.multiple_of(row, SIDE), SIDE), :] += product


def fetched(parts, first, info, tiles, held, sems, transposed):
    copy, chunks = tile_copies(parts, first, info, tiles, held, sems)

    def left_of(part, chunk):
        copy(part, chunk).wait()
        for slot in range(CHUNK):
            number = chunk * CHUNK + slot
            tile = held[part, number]
            yield jnp.concatenate(halves(tile.T if transposed else tile), axis=1), number

    return left_of, chunks


def prepared(tiles):
    def left_of(part, chunk):
        for slot in range(CHUNK):
            number = chunk * CHUNK + slot
            yield tiles[number], number

    return left_of, tiles.shape[0] // CHUNK


def folded(total, nodes):
    live = pl.ds(0, nodes)
    return total[live, :SIDE] + total[live, SIDE:]


def prepare_body(parts, first, transposed, info, tiles, *refs):
    outs, (held, sems) = refs[:parts], refs[parts:]
    left_of, chunks = fetched(parts, first, info, tiles, held, sems, transposed)
    for part in range(parts):

        @pl.loop(0, chunks)
        def _(chunk, part=part):
            for left, number in left_of(part, chunk):
                outs[part][number] = left


def forward_body(n_in, has_start, choose, first, info, *refs):
    panels, tiles = refs[:n_in], refs[n_in]
    out, split, total = refs[n_in + 1 + int(has_start) :][:3]
    nodes, parts = out.shape[0], n_in - int(choose)
    sections = info.shape[0] // 4
    if tiles.dtype == F32:
        left_of, chunks = fetched(parts, first, info, tiles, *refs[-2:], False)
    else:
        left_of, chunks = prepared(tiles)
    total[...] = jnp.zeros_like(total)
    for part in range(parts):
        for block in range(nodes // SIDE):
            at = pl.ds(block * SIDE, SIDE)
            value = panels[part][at, :]
            if choose and part == parts - 1:
                value = jnp.where(info[0, CORE] == 0, value, panels[parts][at, :])
            store_split(split, block, value)
        multiply(
            left_of, part, info[0, first + part], chunks, info, 1 + sections, 1, split, total
        )
    value = folded(total, nodes)
    out[...] = value + refs[n_in + 1][...] if has_start else value


def backward_body(parts, first, info, panel, tiles, *refs):
    outs = refs[:parts]
    split, total = refs[parts : parts + 2]
    nodes = panel.shape[0]
    sections = info.shape[0] // 4
    if tiles.dtype == F32:
        left_of, chunks = fetched(parts, first, info, tiles, *refs[-2:], True)
    else:
        left_of, chunks = prepared(tiles)
    for block in range(nodes // SIDE):
        store_split(split, block, panel[pl.ds(block * SIDE, SIDE), :])
    for part in range(parts):
        total[...] = jnp.zeros_like(total)
        multiply(
            left_of, part, info[0, first + part], chunks, info, 1 + 2 * sections,
            1 + 3 * sections, split, total,
        )
        outs[part][...] = folded(total, nodes)


def local_call(body, parts, slots, info, panels, tiles, extra, outs, scratch):
    whole = pl.BlockSpec(memory_space=pltpu.VMEM)
    raw = tiles.dtype == F32
    if raw:
        scratch = scratch + [
            pltpu.VMEM((parts, slots, SIDE, SIDE), F32),
            pltpu.SemaphoreType.DMA((parts, slots // CHUNK)),
        ]
    return pl.pallas_call(
        body,
        in_specs=[pl.BlockSpec(memory_space=pltpu.SMEM)]
        + [whole] * len(panels)
        + [pl.BlockSpec(memory_space=pltpu.HBM) if raw else whole]
        + [whole] * len(extra),
        out_specs=[whole] * len(outs),
        scratch_shapes=scratch,
        out_shape=outs,
        compiler_params=pltpu.CompilerParams(vmem_limit_bytes=LIMIT << 20),
        cost_estimate=pl.CostEstimate(
            flops=32 * parts * slots * SIDE**3,
            bytes_accessed=4 * parts * slots * SIDE * SIDE,
            transcendentals=0,
        ),
    )(info, *panels, tiles, *extra)


def tile_call(body, parts, info, panels, tiles, extra, n_out):
    nodes, features = panels[0].shape
    return local_call(
        body, parts, tiles.shape[-3], info, panels, tiles, extra,
        [jax.ShapeDtypeStruct((nodes, features), F32)] * n_out,
        [
            pltpu.VMEM((nodes // SIDE, 2 * SIDE, 2 * SIDE), BF16),
            pltpu.VMEM((nodes + SIDE, 2 * features), F32),
        ],
    )


def prepare(parts, first, transposed, info, tiles):
    slots = tiles.shape[1]
    body = functools.partial(prepare_body, parts, first, transposed)
    shape = jax.ShapeDtypeStruct((slots, SIDE, 2 * SIDE), BF16)
    return local_call(body, parts, slots, info, [], tiles, [], [shape] * parts, [])


def forward_tiles(first, info, panels, tiles, start, choose):
    extra = [] if start is None else [start]
    body = functools.partial(forward_body, len(panels), start is not None, choose, first)
    return tile_call(body, len(panels) - int(choose), info, panels, tiles, extra, 1)[0]


def backward_tiles(first, info, panel, tiles, parts):
    body = functools.partial(backward_body, parts, first)
    return tile_call(body, parts, info, [panel], tiles, [], parts)


def widened(value):
    both = jnp.concatenate(halves(value), axis=1)
    return jnp.concatenate([both, both], axis=0)


def split_dot(left, right):
    wide = jnp.dot(
        jnp.concatenate(halves(left), axis=1), widened(right), preferred_element_type=F32
    )
    middle = right.shape[1]
    return wide[:, :middle] + wide[:, middle:]


def dense_body(partials, weight, cotangent, hidden, spread):
    propagated = partials[0]
    for index in range(1, partials.shape[0]):
        propagated = propagated + partials[index]
    preact = split_dot(propagated, weight[...])
    gate = 1.0 / (1.0 + jnp.exp(-preact))
    hidden[...] = preact * gate
    grad_pre = cotangent[...] * gate * (1.0 + preact * (1.0 - gate))
    grad = split_dot(grad_pre, weight[...].T)
    for index in range(spread.shape[0]):
        spread[index] = grad


def dense(partials, weight, cotangent):
    return pl.pallas_call(
        dense_body,
        out_shape=[
            jax.ShapeDtypeStruct(cotangent.shape, F32),
            jax.ShapeDtypeStruct(partials.shape, F32),
        ],
        in_specs=[pl.BlockSpec(memory_space=pltpu.VMEM)] * 3,
        out_specs=[pl.BlockSpec(memory_space=pltpu.VMEM)] * 2,
        compiler_params=pltpu.CompilerParams(vmem_limit_bytes=DENSE_LIMIT << 20),
    )(partials, weight, cotangent)


def shards(features, weight, cotangent, tile_vals, tile_rows, tile_cols, tile_count):
    replicas, groups = lax.axis_size("rep"), lax.axis_size("blk")
    sections = groups // replicas
    rep = lax.axis_index("rep")
    group = lax.axis_index("blk")
    core = group % 2
    tiles, rows, cols, count = tile_vals[0, 0], tile_rows[0, 0], tile_cols[0, 0], tile_count[0, 0]
    slots = rows.shape[-1]
    live = lax.broadcasted_iota(jnp.int32, rows.shape, 1) < count[:, None]
    lane = lax.broadcasted_iota(jnp.int32, (1, slots), 1)
    plan = jnp.where(lane == 0, 2, 0)
    plan = jnp.where(lane == 1, 3 - 2 * core, plan)
    plan = jnp.where(lane == 3, 1 + 2 * core, plan)
    plan = jnp.where(lane == CORE, core, plan)
    spare = replicas
    span, half = groups // 2, replicas // 2
    step = lax.broadcasted_iota(jnp.int32, cols.shape, 0)
    turned = jnp.where((group % span < 2) & (step == 1 - core), half | (half >> 2), 0)
    source = cols ^ rep
    target = source ^ (source >> 2) ^ turned
    info = jnp.concatenate(
        [
            plan,
            jnp.where(live, rows, spare),
            source ^ (rep >> 2) ^ turned,
            rows,
            jnp.where(live, target, spare),
        ]
    )

    def device(group, replica):
        return replica * groups + group % groups

    def joint(block, source):
        return lax.ppermute(
            block, ("rep", "blk"),
            [(device(*source(g, r)), device(g, r)) for r in range(replicas) for g in range(groups)],
        )

    def back(block, target, ids=range(groups)):
        return lax.ppermute(
            block, ("rep", "blk"),
            [(device(g, r), device(*target(g, r))) for r in range(replicas) for g in ids],
        )

    def below(group, replica):
        lower = (group - 2) % groups
        if group % span < 2 and group % 2:
            return lower ^ span, replica ^ half
        return lower, replica

    def along(block, distance, ids):
        return lax.ppermute(block, "blk", [(g, (g + distance) % groups) for g in ids])

    evens, odds = range(0, groups, 2), range(1, groups, 2)
    twin = [(r ^ 1, r) for r in range(replicas)]
    swap = [(g ^ 1, g) for g in range(groups)]

    own = features[0]
    nodes = own.shape[0]
    pair = lax.dynamic_update_slice(
        jnp.concatenate([own, own]), lax.ppermute(own, "rep", twin), (nodes, 0)
    )
    pair, info = lax.optimization_barrier((pair, info))
    low_tiles, rest_tiles = prepare(2, FAR, False, info, tiles)
    base = jnp.concatenate(
        [
            joint(pair, lambda g, r, k=k: (g + sections * r + 2, r ^ (r >> 2) ^ (2 * k)))
            for k in range(replicas // 2)
        ]
    )
    base, low_tiles, rest_tiles = lax.optimization_barrier((base, low_tiles, rest_tiles))
    lower = joint(base, below)
    upper = along(base, -1, evens)
    beside = lax.ppermute(base, "blk", swap)
    partial_sum = forward_tiles(NEAR, info, [base, beside], tiles, None, False)
    lower, partial_sum = lax.optimization_barrier((lower, partial_sum))
    lower_beside = along(lower, -1, odds)
    partial_sum = forward_tiles(FAR, info, [lower], low_tiles, partial_sum, False)
    partial_sum = forward_tiles(
        OUTER, info, [lower_beside, upper], rest_tiles, partial_sum, True
    )
    late_info, partial_sum = lax.optimization_barrier((info, partial_sum))
    (lowest_tiles,) = prepare(1, LOWEST, True, late_info, tiles)
    partials = lax.all_to_all(
        partial_sum.reshape(replicas, -1, own.shape[-1]), "rep", 0, 0, tiled=True
    )
    hidden, spread = dense(partials, weight, cotangent[0])
    grad_panel = lax.all_to_all(spread, "rep", 0, 0, tiled=True).reshape(base.shape)
    (lowest,) = backward_tiles(LOWEST, info, grad_panel, lowest_tiles, 1)
    from_even = back(lowest, below, evens)
    next_panel, lowest = lax.optimization_barrier((grad_panel, lowest))
    (outer,) = backward_tiles(OUTER, info, next_panel, tiles, 1)
    combined = lowest + along(outer, 1, evens)
    from_odd = back(combined, below, odds)
    outer, combined = lax.optimization_barrier((outer, combined))
    to_lower = along(outer, 1, odds)
    late_panel, _ = lax.optimization_barrier((grad_panel, combined))
    (other,) = backward_tiles(NEAR + 1, info, late_panel, tiles, 1)
    late_panel, other = lax.optimization_barrier((late_panel, other))
    (mine,) = backward_tiles(NEAR, info, late_panel, tiles, 1)
    received = lax.optimization_barrier(mine + from_even + to_lower + from_odd)
    total = received + lax.ppermute(other, "blk", swap)
    parts = total.reshape(replicas // 2, -1, own.shape[-1])
    pair_sum = 0.0
    for k in range(replicas // 2):
        part, across = parts[k], (2 * k) ^ (k >> 1)
        if k:
            part = lax.ppermute(part, "rep", [(r, r ^ across) for r in range(replicas)])
        pair_sum = pair_sum + back(
            part, lambda g, r, across=across: (g + sections * (r ^ across) + 2, r)
        )
    kept, sent = jnp.split(pair_sum, 2)
    feature_grad = kept + lax.ppermute(sent, "rep", twin)
    return hidden[None], feature_grad[None]


def solution(mesh):
    placed = (
        P("blk", "rep", None),
        P(),
        P("blk", "rep", None),
        P("blk", "rep", None, None, None, None),
        P("blk", "rep", None, None),
        P("blk", "rep", None, None),
        P("blk", "rep", None),
    )
    return jax.shard_map(
        shards,
        mesh=mesh,
        in_specs=placed,
        out_specs=(P("blk", "rep", None), P("blk", "rep", None)),
        check_vma=False,
    )
```

```python
import functools

import jax
import jax.numpy as jnp
from jax import lax
from jax.experimental import pallas as pl
from jax.experimental.pallas import tpu as pltpu
from jax.sharding import PartitionSpec as P

F32 = jnp.float32
BF16 = jnp.bfloat16
SIDE = 128
CHUNK = 16
LIMIT, DENSE_LIMIT = 48, 16
NEAR, FAR, OUTER, LOWEST, CORE = 0, 2, 3, 2, 4


def halves(value):
    high = value.astype(BF16)
    return high, (value - high.astype(F32)).astype(BF16)


def store_split(split, block, value):
    high, low = halves(value)
    split[block, :SIDE, :SIDE] = high
    split[block, SIDE:, :SIDE] = high
    split[block, :SIDE, SIDE:] = low
    split[block, SIDE:, SIDE:] = low


def tile_copies(parts, first, info, tiles, held, sems):
    chunks = held.shape[1] // CHUNK

    def copy(part, chunk):
        at = pl.ds(pl.multiple_of(chunk * CHUNK, CHUNK), CHUNK)
        return pltpu.make_async_copy(
            tiles.at[info[0, first + part], at], held.at[part, at], sems.at[part, chunk]
        )

    for part in range(parts):
        for chunk in range(chunks):
            copy(part, chunk).start()
    return copy, chunks


def multiply(left_of, part, section, chunks, info, source, target, split, total):
    @pl.loop(0, chunks)
    def _(chunk):
        for left, number in left_of(part, chunk):
            right = split[info[source + section, number]]
            product = jnp.dot(left, right, preferred_element_type=F32)
            row = info[target + section, number] * SIDE
            total[pl.ds(pl.multiple_of(row, SIDE), SIDE), :] += product


def fetched(parts, first, info, tiles, held, sems, transposed):
    copy, chunks = tile_copies(parts, first, info, tiles, held, sems)

    def left_of(part, chunk):
        copy(part, chunk).wait()
        for slot in range(CHUNK):
            number = chunk * CHUNK + slot
            tile = held[part, number]
            yield jnp.concatenate(halves(tile.T if transposed else tile), axis=1), number

    return left_of, chunks


def prepared(tiles):
    def left_of(part, chunk):
        for slot in range(CHUNK):
            number = chunk * CHUNK + slot
            tile = tiles[number]
            if tile.dtype == F32:
                tile = jnp.concatenate(halves(tile.T), axis=1)
            yield tile, number

    return left_of, tiles.shape[0] // CHUNK


def folded(total, nodes):
    live = pl.ds(0, nodes)
    return total[live, :SIDE] + total[live, SIDE:]


def prepare_body(parts, first, transposed, info, tiles, *refs):
    outs, (held, sems) = refs[:parts], refs[parts:]
    left_of, chunks = fetched(parts, first, info, tiles, held, sems, transposed)
    for part in range(parts):

        @pl.loop(0, chunks)
        def _(chunk, part=part):
            for left, number in left_of(part, chunk):
                outs[part][number] = left


def forward_body(n_in, has_start, choose, first, info, *refs):
    panels, tiles = refs[:n_in], refs[n_in]
    out, split, total = refs[n_in + 1 + int(has_start) :][:3]
    nodes, parts = out.shape[0], n_in - int(choose)
    sections = info.shape[0] // 4
    if tiles.dtype == F32:
        left_of, chunks = fetched(parts, first, info, tiles, *refs[-2:], False)
    else:
        left_of, chunks = prepared(tiles)
    total[...] = jnp.zeros_like(total)
    for part in range(parts):
        for block in range(nodes // SIDE):
            at = pl.ds(block * SIDE, SIDE)
            value = panels[part][at, :]
            if choose and part == parts - 1:
                value = jnp.where(info[0, CORE] == 0, value, panels[parts][at, :])
            store_split(split, block, value)
        multiply(
            left_of, part, info[0, first + part], chunks, info, 1 + sections, 1, split, total
        )
    value = folded(total, nodes)
    out[...] = value + refs[n_in + 1][...] if has_start else value


def backward_body(parts, first, ahead, info, panel, tiles, *refs):
    if ahead is not None:
        raw, refs = refs[0], refs[1:]
        following, sem = refs[parts], refs[-1]
        fetch = pltpu.make_async_copy(raw.at[info[0, ahead]], following, sem)
        fetch.start()
    outs = refs[:parts]
    split, total = refs[parts + int(ahead is not None) :][:2]
    nodes = panel.shape[0]
    sections = info.shape[0] // 4
    if len(tiles.shape) == 4:
        left_of, chunks = fetched(parts, first, info, tiles, *refs[-2:], True)
    else:
        left_of, chunks = prepared(tiles)
    for block in range(nodes // SIDE):
        store_split(split, block, panel[pl.ds(block * SIDE, SIDE), :])
    for part in range(parts):
        total[...] = jnp.zeros_like(total)
        multiply(
            left_of, part, info[0, first + part], chunks, info, 1 + 2 * sections,
            1 + 3 * sections, split, total,
        )
        outs[part][...] = folded(total, nodes)
    if ahead is not None:
        fetch.wait()


def local_call(body, parts, slots, info, panels, tiles, extra, outs, scratch):
    whole = pl.BlockSpec(memory_space=pltpu.VMEM)
    raw = len(tiles.shape) == 4
    if raw:
        scratch = scratch + [
            pltpu.VMEM((parts, slots, SIDE, SIDE), F32),
            pltpu.SemaphoreType.DMA((parts, slots // CHUNK)),
        ]
    return pl.pallas_call(
        body,
        in_specs=[pl.BlockSpec(memory_space=pltpu.SMEM)]
        + [whole] * len(panels)
        + [pl.BlockSpec(memory_space=pltpu.HBM) if raw else whole]
        + [pl.BlockSpec(memory_space=pltpu.HBM) if len(e.shape) == 4 else whole for e in extra],
        out_specs=[whole] * len(outs),
        scratch_shapes=scratch,
        out_shape=outs,
        compiler_params=pltpu.CompilerParams(vmem_limit_bytes=LIMIT << 20),
        cost_estimate=pl.CostEstimate(
            flops=32 * parts * slots * SIDE**3,
            bytes_accessed=4 * parts * slots * SIDE * SIDE,
            transcendentals=0,
        ),
    )(info, *panels, tiles, *extra)


def tile_call(body, parts, info, panels, tiles, extra, n_out, ahead=None):
    nodes, features = panels[0].shape
    slots = tiles.shape[-3]
    outs = [jax.ShapeDtypeStruct((nodes, features), F32)] * n_out
    scratch = [
        pltpu.VMEM((nodes // SIDE, 2 * SIDE, 2 * SIDE), BF16),
        pltpu.VMEM((nodes + SIDE, 2 * features), F32),
    ]
    if ahead is not None:
        outs = outs + [jax.ShapeDtypeStruct((slots, SIDE, SIDE), F32)]
        scratch = scratch + [pltpu.SemaphoreType.DMA]
    return local_call(body, parts, slots, info, panels, tiles, extra, outs, scratch)


def prepare(parts, first, transposed, info, tiles):
    slots = tiles.shape[1]
    body = functools.partial(prepare_body, parts, first, transposed)
    shape = jax.ShapeDtypeStruct((slots, SIDE, 2 * SIDE), BF16)
    return local_call(body, parts, slots, info, [], tiles, [], [shape] * parts, [])


def forward_tiles(first, info, panels, tiles, start, choose):
    extra = [] if start is None else [start]
    body = functools.partial(forward_body, len(panels), start is not None, choose, first)
    return tile_call(body, len(panels) - int(choose), info, panels, tiles, extra, 1)[0]


def backward_tiles(first, info, panel, tiles, parts, ahead=None, raw=None):
    body = functools.partial(backward_body, parts, first, ahead)
    extra = [] if ahead is None else [raw]
    return tile_call(body, parts, info, [panel], tiles, extra, parts, ahead)


def widened(value):
    both = jnp.concatenate(halves(value), axis=1)
    return jnp.concatenate([both, both], axis=0)


def split_dot(left, right):
    wide = jnp.dot(
        jnp.concatenate(halves(left), axis=1), widened(right), preferred_element_type=F32
    )
    middle = right.shape[1]
    return wide[:, :middle] + wide[:, middle:]


def dense_body(partials, weight, cotangent, hidden, spread):
    propagated = partials[0]
    for index in range(1, partials.shape[0]):
        propagated = propagated + partials[index]
    preact = split_dot(propagated, weight[...])
    gate = 1.0 / (1.0 + jnp.exp(-preact))
    hidden[...] = preact * gate
    grad_pre = cotangent[...] * gate * (1.0 + preact * (1.0 - gate))
    grad = split_dot(grad_pre, weight[...].T)
    for index in range(spread.shape[0]):
        spread[index] = grad


def dense(partials, weight, cotangent):
    return pl.pallas_call(
        dense_body,
        out_shape=[
            jax.ShapeDtypeStruct(cotangent.shape, F32),
            jax.ShapeDtypeStruct(partials.shape, F32),
        ],
        in_specs=[pl.BlockSpec(memory_space=pltpu.VMEM)] * 3,
        out_specs=[pl.BlockSpec(memory_space=pltpu.VMEM)] * 2,
        compiler_params=pltpu.CompilerParams(vmem_limit_bytes=DENSE_LIMIT << 20),
    )(partials, weight, cotangent)


def shards(features, weight, cotangent, tile_vals, tile_rows, tile_cols, tile_count):
    replicas, groups = lax.axis_size("rep"), lax.axis_size("blk")
    sections = groups // replicas
    rep = lax.axis_index("rep")
    group = lax.axis_index("blk")
    core = group % 2
    tiles, rows, cols, count = tile_vals[0, 0], tile_rows[0, 0], tile_cols[0, 0], tile_count[0, 0]
    slots = rows.shape[-1]
    live = lax.broadcasted_iota(jnp.int32, rows.shape, 1) < count[:, None]
    lane = lax.broadcasted_iota(jnp.int32, (1, slots), 1)
    plan = jnp.where(lane == 0, 2, 0)
    plan = jnp.where(lane == 1, 3 - 2 * core, plan)
    plan = jnp.where(lane == 3, 1 + 2 * core, plan)
    plan = jnp.where(lane == CORE, core, plan)
    spare = replicas
    span, half = groups // 2, replicas // 2
    step = lax.broadcasted_iota(jnp.int32, cols.shape, 0)
    turned = jnp.where((group % span < 2) & (step == 1 - core), half | (half >> 2), 0)
    source = cols ^ rep
    target = source ^ (source >> 2) ^ turned
    info = jnp.concatenate(
        [
            plan,
            jnp.where(live, rows, spare),
            source ^ (rep >> 2) ^ turned,
            rows,
            jnp.where(live, target, spare),
        ]
    )

    def device(group, replica):
        return replica * groups + group % groups

    def joint(block, source):
        return lax.ppermute(
            block, ("rep", "blk"),
            [(device(*source(g, r)), device(g, r)) for r in range(replicas) for g in range(groups)],
        )

    def back(block, target):
        return lax.ppermute(
            block, ("rep", "blk"),
            [(device(g, r), device(*target(g, r))) for r in range(replicas) for g in range(groups)],
        )

    def below(group, replica):
        lower = (group - 2) % groups
        if group % span < 2 and group % 2:
            return lower ^ span, replica ^ half
        return lower, replica

    def along(block, distance, ids):
        return lax.ppermute(block, "blk", [(g, (g + distance) % groups) for g in ids])

    evens, odds = range(0, groups, 2), range(1, groups, 2)
    twin = [(r ^ 1, r) for r in range(replicas)]
    swap = [(g ^ 1, g) for g in range(groups)]

    own = features[0]
    nodes = own.shape[0]
    pair = lax.dynamic_update_slice(
        jnp.concatenate([own, own]), lax.ppermute(own, "rep", twin), (nodes, 0)
    )
    pair, info = lax.optimization_barrier((pair, info))
    low_tiles, rest_tiles = prepare(2, FAR, False, info, tiles)
    base = jnp.concatenate(
        [
            joint(pair, lambda g, r, k=k: (g + sections * r + 2, r ^ (r >> 2) ^ (2 * k)))
            for k in range(replicas // 2)
        ]
    )
    base, low_tiles, rest_tiles = lax.optimization_barrier((base, low_tiles, rest_tiles))
    lower = joint(base, below)
    upper = along(base, -1, evens)
    beside = lax.ppermute(base, "blk", swap)
    partial_sum = forward_tiles(NEAR, info, [base, beside], tiles, None, False)
    lower, partial_sum = lax.optimization_barrier((lower, partial_sum))
    lower_beside = along(lower, -1, odds)
    partial_sum = forward_tiles(FAR, info, [lower], low_tiles, partial_sum, False)
    partial_sum = forward_tiles(
        OUTER, info, [lower_beside, upper], rest_tiles, partial_sum, True
    )
    late_info, partial_sum = lax.optimization_barrier((info, partial_sum))
    (outer_tiles,) = prepare(1, OUTER, True, late_info, tiles)
    partials = lax.all_to_all(
        partial_sum.reshape(replicas, -1, own.shape[-1]), "rep", 0, 0, tiled=True
    )
    hidden, spread = dense(partials, weight, cotangent[0])
    grad_panel = lax.all_to_all(spread, "rep", 0, 0, tiled=True).reshape(base.shape)
    outer, lowest_tiles = backward_tiles(
        OUTER, info, grad_panel, outer_tiles, 1, LOWEST, tiles
    )
    outer_in = along(outer, 1, evens)
    (lowest,) = backward_tiles(LOWEST, info, grad_panel, lowest_tiles, 1)
    combined = lowest + outer_in
    from_upper = back(combined, below)
    outer, combined = lax.optimization_barrier((outer, combined))
    to_lower = along(outer, 1, odds)
    late_panel, _ = lax.optimization_barrier((grad_panel, combined))
    (other,) = backward_tiles(NEAR + 1, info, late_panel, tiles, 1)
    late_panel, other = lax.optimization_barrier((late_panel, other))
    (mine,) = backward_tiles(NEAR, info, late_panel, tiles, 1)
    received = lax.optimization_barrier(mine + from_upper + to_lower)
    total = received + lax.ppermute(other, "blk", swap)
    parts = total.reshape(replicas // 2, -1, own.shape[-1])
    pair_sum = 0.0
    for k in range(replicas // 2):
        part, across = parts[k], (2 * k) ^ (k >> 1)
        if k:
            part = lax.ppermute(part, "rep", [(r, r ^ across) for r in range(replicas)])
        pair_sum = pair_sum + back(
            part, lambda g, r, across=across: (g + sections * (r ^ across) + 2, r)
        )
    kept, sent = jnp.split(pair_sum, 2)
    feature_grad = kept + lax.ppermute(sent, "rep", twin)
    return hidden[None], feature_grad[None]


def solution(mesh):
    placed = (
        P("blk", "rep", None),
        P(),
        P("blk", "rep", None),
        P("blk", "rep", None, None, None, None),
        P("blk", "rep", None, None),
        P("blk", "rep", None, None),
        P("blk", "rep", None),
    )
    return jax.shard_map(
        shards,
        mesh=mesh,
        in_specs=placed,
        out_specs=(P("blk", "rep", None), P("blk", "rep", None)),
        check_vma=False,
    )
```

```python
import functools

import jax
import jax.numpy as jnp
from jax import lax
from jax.experimental import pallas as pl
from jax.experimental.pallas import tpu as pltpu
from jax.sharding import PartitionSpec as P

F32 = jnp.float32
BF16 = jnp.bfloat16
SIDE = 128
CHUNK = 16
LIMIT, DENSE_LIMIT = 48, 16
NEAR, FAR, OUTER, LOWEST, CORE = 0, 2, 3, 2, 4


def halves(value):
    high = value.astype(BF16)
    return high, (value - high.astype(F32)).astype(BF16)


def store_split(split, block, value):
    high, low = halves(value)
    split[block, :SIDE, :SIDE] = high
    split[block, SIDE:, :SIDE] = high
    split[block, :SIDE, SIDE:] = low
    split[block, SIDE:, SIDE:] = low


def tile_copies(parts, first, info, tiles, held, sems):
    chunks = held.shape[1] // CHUNK

    def copy(part, chunk):
        at = pl.ds(pl.multiple_of(chunk * CHUNK, CHUNK), CHUNK)
        return pltpu.make_async_copy(
            tiles.at[info[0, first + part], at], held.at[part, at], sems.at[part, chunk]
        )

    for part in range(parts):
        for chunk in range(chunks):
            copy(part, chunk).start()
    return copy, chunks


def multiply(left_of, part, section, chunks, info, source, target, split, total):
    @pl.loop(0, chunks)
    def _(chunk):
        for left, number in left_of(part, chunk):
            right = split[info[source + section, number]]
            product = jnp.dot(left, right, preferred_element_type=F32)
            row = info[target + section, number] * SIDE
            total[pl.ds(pl.multiple_of(row, SIDE), SIDE), :] += product


def fetched(parts, first, info, tiles, held, sems, transposed):
    copy, chunks = tile_copies(parts, first, info, tiles, held, sems)

    def left_of(part, chunk):
        copy(part, chunk).wait()
        for slot in range(CHUNK):
            number = chunk * CHUNK + slot
            tile = held[part, number]
            yield jnp.concatenate(halves(tile.T if transposed else tile), axis=1), number

    return left_of, chunks


def prepared(tiles):
    def left_of(part, chunk):
        for slot in range(CHUNK):
            number = chunk * CHUNK + slot
            yield tiles[number], number

    return left_of, tiles.shape[0] // CHUNK


def folded(total, nodes):
    live = pl.ds(0, nodes)
    return total[live, :SIDE] + total[live, SIDE:]


def prepare_body(parts, first, transposed, info, tiles, *refs):
    outs, (held, sems) = refs[:parts], refs[parts:]
    left_of, chunks = fetched(parts, first, info, tiles, held, sems, transposed)
    for part in range(parts):

        @pl.loop(0, chunks)
        def _(chunk, part=part):
            for left, number in left_of(part, chunk):
                outs[part][number] = left


def forward_body(n_in, has_start, choose, first, info, *refs):
    panels, tiles = refs[:n_in], refs[n_in]
    out, split, total = refs[n_in + 1 + int(has_start) :][:3]
    nodes, parts = out.shape[0], n_in - int(choose)
    sections = info.shape[0] // 4
    if tiles.dtype == F32:
        left_of, chunks = fetched(parts, first, info, tiles, *refs[-2:], False)
    else:
        left_of, chunks = prepared(tiles)
    total[...] = jnp.zeros_like(total)
    for part in range(parts):
        for block in range(nodes // SIDE):
            at = pl.ds(block * SIDE, SIDE)
            value = panels[part][at, :]
            if choose and part == parts - 1:
                value = jnp.where(info[0, CORE] == 0, value, panels[parts][at, :])
            store_split(split, block, value)
        multiply(
            left_of, part, info[0, first + part], chunks, info, 1 + sections, 1, split, total
        )
    value = folded(total, nodes)
    out[...] = value + refs[n_in + 1][...] if has_start else value


def backward_body(parts, first, info, panel, tiles, *refs):
    outs = refs[:parts]
    split, total = refs[parts : parts + 2]
    nodes = panel.shape[0]
    sections = info.shape[0] // 4
    if tiles.dtype == F32:
        left_of, chunks = fetched(parts, first, info, tiles, *refs[-2:], True)
    else:
        left_of, chunks = prepared(tiles)
    for block in range(nodes // SIDE):
        store_split(split, block, panel[pl.ds(block * SIDE, SIDE), :])
    for part in range(parts):
        total[...] = jnp.zeros_like(total)
        multiply(
            left_of, part, info[0, first + part], chunks, info, 1 + 2 * sections,
            1 + 3 * sections, split, total,
        )
        outs[part][...] = folded(total, nodes)


def local_call(body, parts, slots, info, panels, tiles, extra, outs, scratch):
    whole = pl.BlockSpec(memory_space=pltpu.VMEM)
    raw = tiles.dtype == F32
    if raw:
        scratch = scratch + [
            pltpu.VMEM((parts, slots, SIDE, SIDE), F32),
            pltpu.SemaphoreType.DMA((parts, slots // CHUNK)),
        ]
    return pl.pallas_call(
        body,
        in_specs=[pl.BlockSpec(memory_space=pltpu.SMEM)]
        + [whole] * len(panels)
        + [pl.BlockSpec(memory_space=pltpu.HBM) if raw else whole]
        + [whole] * len(extra),
        out_specs=[whole] * len(outs),
        scratch_shapes=scratch,
        out_shape=outs,
        compiler_params=pltpu.CompilerParams(vmem_limit_bytes=LIMIT << 20),
        cost_estimate=pl.CostEstimate(
            flops=32 * parts * slots * SIDE**3,
            bytes_accessed=4 * parts * slots * SIDE * SIDE,
            transcendentals=0,
        ),
    )(info, *panels, tiles, *extra)


def tile_call(body, parts, info, panels, tiles, extra, n_out):
    nodes, features = panels[0].shape
    return local_call(
        body, parts, tiles.shape[-3], info, panels, tiles, extra,
        [jax.ShapeDtypeStruct((nodes, features), F32)] * n_out,
        [
            pltpu.VMEM((nodes // SIDE, 2 * SIDE, 2 * SIDE), BF16),
            pltpu.VMEM((nodes + SIDE, 2 * features), F32),
        ],
    )


def prepare(parts, first, transposed, info, tiles):
    slots = tiles.shape[1]
    body = functools.partial(prepare_body, parts, first, transposed)
    shape = jax.ShapeDtypeStruct((slots, SIDE, 2 * SIDE), BF16)
    return local_call(body, parts, slots, info, [], tiles, [], [shape] * parts, [])


def forward_tiles(first, info, panels, tiles, start, choose):
    extra = [] if start is None else [start]
    body = functools.partial(forward_body, len(panels), start is not None, choose, first)
    return tile_call(body, len(panels) - int(choose), info, panels, tiles, extra, 1)[0]


def backward_tiles(first, info, panel, tiles, parts):
    body = functools.partial(backward_body, parts, first)
    return tile_call(body, parts, info, [panel], tiles, [], parts)


def widened(value):
    both = jnp.concatenate(halves(value), axis=1)
    return jnp.concatenate([both, both], axis=0)


def split_dot(left, right):
    wide = jnp.dot(
        jnp.concatenate(halves(left), axis=1), widened(right), preferred_element_type=F32
    )
    middle = right.shape[1]
    return wide[:, :middle] + wide[:, middle:]


def dense_body(partials, weight, cotangent, hidden, spread):
    propagated = partials[0]
    for index in range(1, partials.shape[0]):
        propagated = propagated + partials[index]
    preact = split_dot(propagated, weight[...])
    gate = 1.0 / (1.0 + jnp.exp(-preact))
    hidden[...] = preact * gate
    grad_pre = cotangent[...] * gate * (1.0 + preact * (1.0 - gate))
    grad = split_dot(grad_pre, weight[...].T)
    for index in range(spread.shape[0]):
        spread[index] = grad


def dense(partials, weight, cotangent):
    return pl.pallas_call(
        dense_body,
        out_shape=[
            jax.ShapeDtypeStruct(cotangent.shape, F32),
            jax.ShapeDtypeStruct(partials.shape, F32),
        ],
        in_specs=[pl.BlockSpec(memory_space=pltpu.VMEM)] * 3,
        out_specs=[pl.BlockSpec(memory_space=pltpu.VMEM)] * 2,
        compiler_params=pltpu.CompilerParams(vmem_limit_bytes=DENSE_LIMIT << 20),
    )(partials, weight, cotangent)


def shards(features, weight, cotangent, tile_vals, tile_rows, tile_cols, tile_count):
    replicas, groups = lax.axis_size("rep"), lax.axis_size("blk")
    sections = groups // replicas
    rep = lax.axis_index("rep")
    group = lax.axis_index("blk")
    core = group % 2
    tiles, rows, cols, count = tile_vals[0, 0], tile_rows[0, 0], tile_cols[0, 0], tile_count[0, 0]
    slots = rows.shape[-1]
    live = lax.broadcasted_iota(jnp.int32, rows.shape, 1) < count[:, None]
    lane = lax.broadcasted_iota(jnp.int32, (1, slots), 1)
    plan = jnp.where(lane == 0, 2, 0)
    plan = jnp.where(lane == 1, 3 - 2 * core, plan)
    plan = jnp.where(lane == 3, 1 + 2 * core, plan)
    plan = jnp.where(lane == CORE, core, plan)
    spare = replicas
    span, half = groups // 2, replicas // 2
    step = lax.broadcasted_iota(jnp.int32, cols.shape, 0)
    turned = jnp.where((group % span < 2) & (step == 1 - core), half | (half >> 2), 0)
    source = cols ^ rep
    target = source ^ (source >> 2) ^ turned
    info = jnp.concatenate(
        [
            plan,
            jnp.where(live, rows, spare),
            source ^ (rep >> 2) ^ turned,
            rows,
            jnp.where(live, target, spare),
        ]
    )

    def device(group, replica):
        return replica * groups + group % groups

    def joint(block, source):
        return lax.ppermute(
            block, ("rep", "blk"),
            [(device(*source(g, r)), device(g, r)) for r in range(replicas) for g in range(groups)],
        )

    def back(block, target):
        return lax.ppermute(
            block, ("rep", "blk"),
            [(device(g, r), device(*target(g, r))) for r in range(replicas) for g in range(groups)],
        )

    def below(group, replica):
        lower = (group - 2) % groups
        if group % span < 2 and group % 2:
            return lower ^ span, replica ^ half
        return lower, replica

    def along(block, distance, ids):
        return lax.ppermute(block, "blk", [(g, (g + distance) % groups) for g in ids])

    evens, odds = range(0, groups, 2), range(1, groups, 2)
    twin = [(r ^ 1, r) for r in range(replicas)]
    swap = [(g ^ 1, g) for g in range(groups)]

    own = features[0]
    nodes = own.shape[0]
    pair = lax.dynamic_update_slice(
        jnp.concatenate([own, own]), lax.ppermute(own, "rep", twin), (nodes, 0)
    )
    pair, info = lax.optimization_barrier((pair, info))
    low_tiles, rest_tiles = prepare(2, FAR, False, info, tiles)
    base = jnp.concatenate(
        [
            joint(pair, lambda g, r, k=k: (g + sections * r + 2, r ^ (r >> 2) ^ (2 * k)))
            for k in range(replicas // 2)
        ]
    )
    base, low_tiles, rest_tiles = lax.optimization_barrier((base, low_tiles, rest_tiles))
    lower = joint(base, below)
    upper = along(base, -1, evens)
    beside = lax.ppermute(base, "blk", swap)
    partial_sum = forward_tiles(NEAR, info, [base, beside], tiles, None, False)
    lower, partial_sum = lax.optimization_barrier((lower, partial_sum))
    lower_beside = along(lower, -1, odds)
    partial_sum = forward_tiles(FAR, info, [lower], low_tiles, partial_sum, False)
    partial_sum = forward_tiles(
        OUTER, info, [lower_beside, upper], rest_tiles, partial_sum, True
    )
    late_info, partial_sum = lax.optimization_barrier((info, partial_sum))
    (outer_tiles,) = prepare(1, OUTER, True, late_info, tiles)
    partials = lax.all_to_all(
        partial_sum.reshape(replicas, -1, own.shape[-1]), "rep", 0, 0, tiled=True
    )
    hidden, spread = dense(partials, weight, cotangent[0])
    grad_panel = lax.all_to_all(spread, "rep", 0, 0, tiled=True).reshape(base.shape)
    (outer,) = backward_tiles(OUTER, info, grad_panel, outer_tiles, 1)
    outer_in = along(outer, 1, evens)
    (lowest,) = backward_tiles(LOWEST, info, grad_panel, tiles, 1)
    combined = lowest + outer_in
    from_upper = back(combined, below)
    outer, combined = lax.optimization_barrier((outer, combined))
    to_lower = along(outer, 1, odds)
    late_panel, _ = lax.optimization_barrier((grad_panel, combined))
    (other,) = backward_tiles(NEAR + 1, info, late_panel, tiles, 1)
    late_panel, other = lax.optimization_barrier((late_panel, other))
    (mine,) = backward_tiles(NEAR, info, late_panel, tiles, 1)
    received = lax.optimization_barrier(mine + from_upper + to_lower)
    total = received + lax.ppermute(other, "blk", swap)
    parts = total.reshape(replicas // 2, -1, own.shape[-1])
    pair_sum = 0.0
    for k in reversed(range(replicas // 2)):
        part, across = parts[k], (2 * k) ^ (k >> 1)
        if k:
            part = lax.ppermute(part, "rep", [(r, r ^ across) for r in range(replicas)])
        pair_sum = pair_sum + back(
            part, lambda g, r, across=across: (g + sections * (r ^ across) + 2, r)
        )
    kept, sent = jnp.split(pair_sum, 2)
    feature_grad = kept + lax.ppermute(sent, "rep", twin)
    return hidden[None], feature_grad[None]


def solution(mesh):
    placed = (
        P("blk", "rep", None),
        P(),
        P("blk", "rep", None),
        P("blk", "rep", None, None, None, None),
        P("blk", "rep", None, None),
        P("blk", "rep", None, None),
        P("blk", "rep", None),
    )
    return jax.shard_map(
        shards,
        mesh=mesh,
        in_specs=placed,
        out_specs=(P("blk", "rep", None), P("blk", "rep", None)),
        check_vma=False,
    )
```
